512 devices in a mesh: dp: 16 (over z), mem: 32 (over x, y, core).
Axes of the slice: x: 4, y: 4, z: 16, core: 2. Of those that a mesh axis runs over, the one named last changes fastest.
Arguments:
- owners: int32 [65536, 3], P(('dp', 'mem')), may hold values from 0 to 31, as said below
- pick_index: int32 [65536, 32], P(('dp', 'mem')), may hold values from 0 to 95, as said below
- key_scores: float32 [65536, 32], P(('dp', 'mem')), may hold values from -12 to 320
- output_cotangent: bfloat16 [65536, 4096], P(('dp', 'mem')), may hold values from -0.5 to 0.5
- value_table: bfloat16 [1024, 4096], P('mem'), may hold values from -14 to 14
- first_moment: float32 [1024, 4096], P('mem'), may hold values from -3 to 3
- second_moment: float32 [1024, 4096], P('mem'), may hold values from 0.5 to 8
- norm_gain: float32 [4096], replicated, may hold values from 0.5 to 1.5
Outputs:
- memory_out: bfloat16 [65536, 4096], P(('dp', 'mem'))
- score_gradient: float32 [65536, 32], P(('dp', 'mem'))
- gain_gradient: float32 [4096], replicated
- updated_table: bfloat16 [1024, 4096], P('mem')
- updated_first: float32 [1024, 4096], P('mem')
- updated_second: float32 [1024, 4096], P('mem')
The draws below stay inside these ranges and needn't reach their ends.
Inputs may be any that keep to these rules, and one draw needn't show every extreme that they name: Each token names 3 different owners. Within the tokens of one device (aligned blocks of 128 rows) no owner is named by more than 24 tokens, and one owner, the same for every block of a draw, is named by exactly 24 tokens of every block. `pick_index`: the 32 entries of a token are different.
All inputs are finite; a program needn't handle non-finite values.
Results may differ from the reference program's by a relative error of at most 0.006.
Values may be sent and summed in bfloat16 or wider, within the bound.
No kernel may reach another device: no remote copies, remote signals or barrier semaphores. Data moves between devices by JAX's collectives and lax.ppermute only.
A program may use at most 64 MiB of HBM per device.

```python
import math
import jax
import jax.numpy as jnp
from jax import lax

D = 4096
TOPK = 32
CANDS = 3
TOK_DEV = 128
ROWS_DEV = 32
TOKENS = 65536
TABLE_ROWS = 1024
CAP = 24


def block_owners(block_key, hot_owner):
    others_count = TABLE_ROWS // ROWS_DEV - 1
    owner_total = others_count + 1
    pair_total = CANDS * TOK_DEV
    remaining = pair_total - CAP
    rank_list = jnp.arange(others_count, dtype=jnp.int32)
    rank_weight = others_count + 2 * (others_count - 1 - rank_list)
    base_load = remaining * rank_weight // (others_count * (2 * others_count - 1))
    leftover = remaining - jnp.sum(base_load)
    base_load = base_load + (rank_list >= others_count - leftover).astype(jnp.int32)
    pair_half = others_count // 2
    shift_key, order_key, token_key = jax.random.split(block_key, 3)
    moved_count = jax.random.randint(shift_key, (pair_half,), 0, 2).astype(jnp.int32)
    moved_count = jnp.minimum(moved_count, base_load[0:2 * pair_half:2])
    move_list = jnp.stack([-moved_count, moved_count], axis=1).reshape(2 * pair_half)
    move_list = jnp.concatenate([move_list, jnp.zeros((others_count - 2 * pair_half,), jnp.int32)])
    load_rank = base_load + move_list
    others = (hot_owner + 1 + jax.random.permutation(order_key, others_count).astype(jnp.int32)) % owner_total
    owner_list = jnp.concatenate([jnp.reshape(hot_owner, (1,)), others])
    load_list = jnp.concatenate([jnp.full((1,), CAP, jnp.int32), load_rank])
    run_ends = jnp.cumsum(load_list)
    positions = jnp.arange(pair_total, dtype=jnp.int32)
    run_index = jnp.sum((positions[:, None] >= run_ends[None, :]).astype(jnp.int32), axis=1)
    sequence = jnp.take(owner_list, run_index)
    chosen = sequence.reshape(CANDS, TOK_DEV).T
    return jnp.take(chosen, jax.random.permutation(token_key, TOK_DEV), axis=0)


def draw_owners(key, part):
    key = jax.random.fold_in(key, 11)
    hot_owner = jax.random.randint(jax.random.fold_in(key, 0), (), 0, TABLE_ROWS // ROWS_DEV).astype(jnp.int32)
    block_keys = jax.random.split(jax.random.fold_in(key, 1), TOKENS // TOK_DEV)
    blocks = jax.vmap(block_owners, in_axes=(0, None))(block_keys, hot_owner)
    return blocks.reshape(TOKENS, CANDS).astype(jnp.int32)


def one_token(token_key):
    return jax.random.permutation(token_key, CANDS * ROWS_DEV)[:TOPK].astype(jnp.int32)


def draw_pick_index(key, part):
    key = jax.random.fold_in(key, 12)
    return jax.vmap(one_token)(jax.random.split(key, TOKENS))


def draw_key_scores(key, part):
    key = jax.random.fold_in(key, 13)
    base_key = jax.random.fold_in(key, 0)
    return jnp.clip(3.0 * jax.random.normal(base_key, (TOKENS, TOPK), jnp.float32), -9.0, 9.0)


def draw_value_table(key, part):
    key = jax.random.fold_in(key, 14)
    entry_key, row_key, column_key = jax.random.split(key, 3)
    row_scale = jnp.exp(jax.random.uniform(row_key, (TABLE_ROWS, 1), jnp.float32, 0.0, 1.1513))
    column_scale = jnp.exp(jax.random.uniform(column_key, (1, D), jnp.float32, 0.0, 1.1513))
    entries = jnp.clip(jax.random.normal(entry_key, (TABLE_ROWS, D), jnp.float32), -4.0, 4.0)
    return (entries * row_scale * column_scale / 3.0).astype(jnp.bfloat16)


def steps_of(rng, extent, shards, low, top_value):
    def one(position, parts):
        heights = jax.random.uniform(jax.random.fold_in(jax.random.fold_in(rng, 6), position), (parts,), jnp.float32, low / len(shards), top_value / len(shards))
        return jnp.repeat(jnp.exp(heights), extent[position] // parts).reshape((-1,) + (1,) * (len(extent) - position - 1))

    factor_of = one(*shards[0])
    for cut in shards[1:]:
        factor_of = factor_of * one(*cut)
    return factor_of


def scatter_about(key, shape, scale, most, cuts=(), kind=jnp.bfloat16):
    loudness = steps_of(key, shape, cuts, -0.22, 0.18) if cuts else 1.0
    array = jax.random.normal(key, shape, jnp.float32) * scale * loudness
    return jnp.minimum(jnp.maximum(array, -most), most).astype(kind)


def setup_inputs(seed: int = 0) -> dict:
    keys = jax.random.split(jax.random.key(seed), 9)
    return {
        "owners": draw_owners(jax.random.fold_in(keys[8], 71), 0),
        "pick_index": draw_pick_index(jax.random.fold_in(keys[8], 71), 0),
        "key_scores": draw_key_scores(jax.random.fold_in(keys[8], 71), 0),
        "output_cotangent": scatter_about(keys[3], (TOKENS, D), 0.0625, 0.5, ((0, 512),)),
        "value_table": draw_value_table(jax.random.fold_in(keys[8], 71), 0),
        "first_moment": scatter_about(keys[5], (TABLE_ROWS, D), 0.5, 3.0, ((0, 32),), jnp.float32),
        "second_moment": jnp.clip(jnp.exp(math.log(8.0) - 2.7725887 * jax.random.uniform(keys[6], (TABLE_ROWS, D), jnp.float32) ** steps_of(keys[6], (TABLE_ROWS, D), ((0, 32),), -0.2, 0.2)), 0.5, 8.0),
        "norm_gain": jnp.clip(1.0 + 0.1 * jax.random.normal(keys[7], (D,), jnp.float32), 0.5, 1.5),
    }


beta_first = 0.9
beta_second = 0.95
learning_rate = 0.01
adam_epsilon = 1e-08
first_bias = 1.0 - (0.9 ** 50) ** 2
second_bias = 1.0 - (0.95 ** 50) ** 2
norm_epsilon = 1e-05

def token_block(value_table, norm_gain, blocks):
    owners, pick_index, key_scores, output_cotangent = blocks
    weights = jax.nn.softmax(key_scores.astype(jnp.float32), axis=-1)
    spread = (pick_index[:, :, None] == jnp.arange(CANDS * ROWS_DEV, dtype=jnp.int32)[None, None, :]).astype(jnp.float32)
    placed = jnp.einsum('tkm,tk->tm', spread, weights, precision=lax.Precision.HIGHEST)
    placed = lax.optimization_barrier(placed.astype(jnp.bfloat16)).astype(jnp.float32)
    placed = placed.reshape(-1, CANDS, ROWS_DEV)
    grouped = value_table.reshape(TABLE_ROWS // ROWS_DEV, ROWS_DEV, D)
    rows_used = grouped[owners].astype(jnp.float32)
    partial_value = jnp.einsum('tcj,tcjd->tcd', placed, rows_used)
    partial_value = lax.optimization_barrier(partial_value.astype(jnp.bfloat16)).astype(jnp.float32)
    memory = lax.optimization_barrier(jnp.sum(partial_value, axis=1))
    inverse = lax.rsqrt(lax.optimization_barrier(jnp.mean(memory * memory, axis=-1, keepdims=True)) + norm_epsilon)
    gain_row = norm_gain.astype(jnp.float32)
    memory_out = (memory * inverse * gain_row).astype(jnp.bfloat16)
    cotangent = output_cotangent.astype(jnp.float32)
    scaled = cotangent * gain_row
    memory_grad = inverse * scaled - memory * inverse ** 3 * lax.optimization_barrier(jnp.mean(scaled * memory, axis=-1, keepdims=True))
    memory_grad = lax.optimization_barrier(memory_grad.astype(jnp.bfloat16)).astype(jnp.float32)
    gain_part = lax.optimization_barrier(jnp.sum(cotangent * memory * inverse, axis=0))
    placed_grad = jnp.einsum('td,tcjd->tcj', memory_grad, rows_used).reshape(-1, CANDS * ROWS_DEV)
    weight_grad = jnp.einsum('tkm,tm->tk', spread, placed_grad, precision=lax.Precision.HIGHEST)
    score_gradient = weights * (weight_grad - lax.optimization_barrier(jnp.sum(weights * weight_grad, axis=-1, keepdims=True)))
    row_terms = jnp.einsum('tcj,td->tcjd', placed, memory_grad)
    table_part = jnp.zeros((TABLE_ROWS // ROWS_DEV, ROWS_DEV, D), jnp.float32).at[owners].add(row_terms)
    return (memory_out, score_gradient, table_part, gain_part)

def reference(owners, pick_index, key_scores, output_cotangent, value_table, first_moment, second_moment, norm_gain):
    block_count = TOKENS // TOK_DEV
    stacked = (owners.reshape(block_count, TOK_DEV, CANDS), pick_index.reshape(block_count, TOK_DEV, TOPK), key_scores.reshape(block_count, TOK_DEV, TOPK), output_cotangent.reshape(block_count, TOK_DEV, D))

    def advance(running, blocks):
        table_sum, gain_sum = running
        memory_out, score_gradient, table_part, gain_part = token_block(value_table, norm_gain, blocks)
        return ((table_sum + table_part, gain_sum + gain_part), (memory_out, score_gradient))
    initial = (jnp.zeros((TABLE_ROWS // ROWS_DEV, ROWS_DEV, D), jnp.float32), jnp.zeros((D,), jnp.float32))
    (table_sum, gain_gradient), (memory_out, score_gradient) = lax.scan(advance, initial, stacked)
    gradient = table_sum.reshape(TABLE_ROWS, D)
    updated_first = beta_first * first_moment + (1.0 - beta_first) * gradient
    updated_second = beta_second * second_moment + (1.0 - beta_second) * gradient * gradient
    update = learning_rate * (updated_first / first_bias) / (jnp.sqrt(updated_second / second_bias) + adam_epsilon)
    updated_table = (value_table.astype(jnp.float32) - update).astype(jnp.bfloat16)
    return (memory_out.reshape(TOKENS, D), score_gradient.reshape(TOKENS, TOPK), gain_gradient, updated_table, updated_first, updated_second)
```

```python
import functools

import jax
import jax.numpy as jnp
from jax import lax
from jax.experimental import pallas as pl
from jax.experimental.pallas import tpu as pltpu
from jax.sharding import Mesh
from jax.sharding import PartitionSpec as P

beta_first = 0.9
beta_second = 0.95
learning_rate = 0.01
adam_epsilon = 1e-08
first_bias = 1.0 - (0.9**50) ** 2
second_bias = 1.0 - (0.95**50) ** 2
norm_epsilon = 1e-05

L = 128
PAIR = 2
RING = 8
GROUP = PAIR * RING
CANDS = 3
ROWS = 32
PICKS = 32
D = 4096
WIDE = D // GROUP
TILES = WIDE // L
TOK = 128
SLOTS = CANDS * ROWS
TABLE = 1024
OWNERS = TABLE // ROWS
INFO = SLOTS + 8
GAIN_AT = TILES * ROWS
GRAD = GAIN_AT + 8
BACK = WIDE + SLOTS
STEP = 2
VMEM_LIMIT = 32 * 1024 * 1024
F32 = jnp.float32
BF16 = jnp.bfloat16
PARAMS = pltpu.CompilerParams(vmem_limit_bytes=VMEM_LIMIT)


def dot(a, b, dims):
    return lax.dot_general(a, b, (dims, ((), ())), preferred_element_type=F32)


def shape(*dims_and_type):
    return jax.ShapeDtypeStruct(dims_and_type[:-1], dims_and_type[-1])


def in_hbm(*dims_and_type):
    return pltpu.HBM(dims_and_type[:-1], dims_and_type[-1])


def table_kernel(place_ref, table_ref, out_ref):
    del place_ref
    for j in range(TILES):
        tile = table_ref[:, j * L : (j + 1) * L]
        for x in range(out_ref.shape[0]):
            out_ref[x, 0, j * ROWS : (j + 1) * ROWS, :] = tile


def pack_kernel(owners_ref, pick_ref, scores_ref, cotangent_ref, send_ref, weights_ref, info_ref):
    @pl.when(pl.program_id(0) == 0)
    def _():
        scores = scores_ref[...]
        shifted = jnp.exp(scores - jnp.max(scores, axis=0, keepdims=True))
        weights = shifted / jnp.sum(shifted, axis=0, keepdims=True)
        weights_ref[...] = weights
        pick = pick_ref[...]
        entry = lax.broadcasted_iota(jnp.int32, (SLOTS, TOK), 0)
        placed = jnp.zeros((SLOTS, TOK), F32)
        for k in range(PICKS):
            placed = jnp.where(pick[k : k + 1] == entry, weights[k : k + 1], placed)
        owners = owners_ref[...].astype(F32)
        line = lax.broadcasted_iota(jnp.int32, (8, TOK), 0)
        named = jnp.zeros((8, TOK), F32)
        for c in range(CANDS):
            named = jnp.where(line == c, owners[c : c + 1], named)
        info_ref[...] = jnp.concatenate([placed, named], axis=0).astype(BF16)

    for j in range(TILES):
        send_ref[0, j * L : (j + 1) * L, :] = jnp.transpose(cotangent_ref[:, j * L : (j + 1) * L])
    send_ref[0, WIDE:, :] = info_ref[...]


def load_info(batch_ref):
    info = jnp.concatenate([batch_ref[i, WIDE:, :] for i in range(STEP)], axis=1).astype(F32)
    placed = [info[c * ROWS : (c + 1) * ROWS] for c in range(CANDS)]
    named = [
        jnp.broadcast_to(info[SLOTS + c : SLOTS + c + 1], (ROWS, STEP * TOK)) for c in range(CANDS)
    ]
    return placed, named


def place(placed, named):
    blocks = []
    for o in range(OWNERS):
        block = jnp.zeros((ROWS, STEP * TOK), F32)
        for c in range(CANDS):
            block = jnp.where(named[c] == float(o), placed[c], block)
        blocks.append(block.astype(BF16))
    return jnp.concatenate(blocks, axis=0)


def load_table(table_ref):
    return jnp.concatenate(
        [table_ref[:, j * ROWS : (j + 1) * ROWS, :].reshape(TABLE, L) for j in range(TILES)], axis=1
    )


def load_cotangent(batch_ref):
    return jnp.concatenate([batch_ref[i, :WIDE, :] for i in range(STEP)], axis=1).astype(F32)


def forward_kernel(batch_ref, table_ref, gain_ref, memory_ref, sums_ref, turned_ref):
    @pl.when(pl.program_id(0) == 0)
    def _():
        turned_ref[...] = jnp.transpose(load_table(table_ref))

    memory = dot(turned_ref[...], place(*load_info(batch_ref)), ((1,), (0,)))
    memory_ref[...] = memory
    scaled = load_cotangent(batch_ref) * gain_ref[...]
    square = jnp.sum(memory * memory, axis=0, keepdims=True)
    cross = jnp.sum(scaled * memory, axis=0, keepdims=True)
    both = jnp.concatenate([square, cross], axis=0)
    for g in range(sums_ref.shape[0]):
        sums_ref[g] = both


def split(value):
    high = value.astype(BF16).astype(F32)
    return high, value - high


def gain_rows(rows):
    high, low = split(rows)
    return jnp.concatenate([high, low, jnp.zeros((8 - 2 * TILES, L), F32)], axis=0).astype(BF16)


def backward_kernel(batch_ref, gain_ref, memory_ref, sums_ref, out_ref, grad_ref, send_ref, total_ref, gain_sum_ref):
    step = pl.program_id(0)
    sums = jnp.sum(sums_ref[...], axis=0)
    inverse = lax.rsqrt(sums[0:1] / D + norm_epsilon)
    factor = inverse * inverse * inverse * (sums[1:2] / D)
    memory = memory_ref[...]
    cotangent = load_cotangent(batch_ref)
    gain = gain_ref[...]
    normed = memory * inverse
    out_ref[...] = (normed * gain).astype(BF16)
    grad = (inverse * (cotangent * gain) - memory * factor).astype(BF16)
    grad_ref[...] = grad
    gain_part = cotangent * normed
    folded = sum(gain_part[:, i * L : (i + 1) * L] for i in range(STEP))
    table_part = dot(place(*load_info(batch_ref)), grad, ((1,), (1,)))

    @pl.when(step == 0)
    def _():
        total_ref[...] = table_part
        gain_sum_ref[...] = folded

    @pl.when(step > 0)
    def _():
        total_ref[...] += table_part
        gain_sum_ref[...] += folded

    @pl.when(step == pl.num_programs(0) - 1)
    def _():
        for j in range(TILES):
            send_ref[:, j * ROWS : (j + 1) * ROWS, :] = (
                total_ref[:, j * L : (j + 1) * L].astype(BF16).reshape(OWNERS, ROWS, L)
            )
        turned = jnp.transpose(gain_sum_ref[...])
        rows = [jnp.sum(turned[:, j * L : (j + 1) * L], axis=0, keepdims=True) for j in range(TILES)]
        tail = gain_rows(jnp.concatenate(rows, axis=0))
        for o in range(OWNERS):
            send_ref[o, GAIN_AT:, :] = tail


def placed_grad_kernel(batch_ref, table_ref, out_ref, grad_ref, send_ref):
    _, named = load_info(batch_ref)
    full = dot(load_table(table_ref), grad_ref[...], ((1,), (0,)))
    found = [jnp.zeros((ROWS, STEP * TOK), F32) for _ in range(CANDS)]
    for o in range(OWNERS):
        block = full[o * ROWS : (o + 1) * ROWS]
        for c in range(CANDS):
            found[c] = jnp.where(named[c] == float(o), block, found[c])
    for i in range(STEP):
        send_ref[i, :WIDE, :] = out_ref[:, i * TOK : (i + 1) * TOK]
        for c in range(CANDS):
            send_ref[i, WIDE + c * ROWS : WIDE + (c + 1) * ROWS, :] = found[c][
                :, i * TOK : (i + 1) * TOK
            ].astype(BF16)


def merge(parts):
    total = jnp.sum(parts, axis=0)
    gain = total[GAIN_AT : GAIN_AT + TILES] + total[GAIN_AT + TILES : GAIN_AT + 2 * TILES]
    return total[:GAIN_AT], gain


def plane_kernel(parts_ref, send_ref):
    for b in range(parts_ref.shape[1]):
        rows, gain = merge(parts_ref[:, b].astype(F32))
        send_ref[b, :GAIN_AT, :] = rows.astype(BF16)
        send_ref[b, GAIN_AT:, :] = gain_rows(gain)


def share_kernel(parts_ref, send_ref):
    rows, gain = merge(parts_ref[...].astype(F32))
    rows = rows.astype(BF16)
    tail = gain_rows(gain)
    for b in range(send_ref.shape[0]):
        send_ref[b, :GAIN_AT, :] = rows
        send_ref[b, GAIN_AT:, :] = tail


def adam_kernel(grad_ref, table_ref, first_ref, second_ref, new_table_ref, new_first_ref, new_second_ref, gain_ref):
    for b in range(grad_ref.shape[0]):
        for j in range(TILES):
            at = b * WIDE + j * L
            grad = grad_ref[b, j * ROWS : (j + 1) * ROWS, :].astype(F32)
            first = beta_first * first_ref[:, at : at + L] + (1.0 - beta_first) * grad
            second = beta_second * second_ref[:, at : at + L] + (1.0 - beta_second) * grad * grad
            update = learning_rate * (first / first_bias) / (jnp.sqrt(second / second_bias) + adam_epsilon)
            new_first_ref[:, at : at + L] = first
            new_second_ref[:, at : at + L] = second
            new_table_ref[:, at : at + L] = (table_ref[:, at : at + L].astype(F32) - update).astype(BF16)
            tail = grad_ref[b, GAIN_AT:, :].astype(F32)
            gain_ref[:, at : at + L] = tail[j : j + 1] + tail[TILES + j : TILES + j + 1]


def out_kernel(parts_ref, pick_ref, weights_ref, out_ref, score_ref, placed_grad_ref):
    step = pl.program_id(0)
    for j in range(TILES):
        out_ref[:, j * L : (j + 1) * L] = jnp.transpose(parts_ref[0, j * L : (j + 1) * L, :])
    part = parts_ref[0, WIDE:, :].astype(F32)

    @pl.when(step == 0)
    def _():
        placed_grad_ref[...] = part

    @pl.when(step > 0)
    def _():
        placed_grad_ref[...] += part

    @pl.when(step == pl.num_programs(0) - 1)
    def _():
        pick = pick_ref[...]
        weights = weights_ref[...]
        weight_grad = jnp.zeros((PICKS, TOK), F32)
        for m in range(SLOTS):
            weight_grad = jnp.where(pick == m, placed_grad_ref[m : m + 1, :], weight_grad)
        mean = jnp.sum(weights * weight_grad, axis=0, keepdims=True)
        score_ref[...] = weights * (weight_grad - mean)


def exchange(array, axes):
    return lax.all_to_all(array, axes, split_axis=0, concat_axis=0, tiled=True)


def per_device(
    owners,
    pick_index,
    key_scores,
    output_cotangent,
    value_table,
    first_moment,
    second_moment,
    norm_gain,
):
    rows_x = lax.axis_size("x")
    steps = GROUP // STEP
    half = lax.axis_index("dl")
    block_index = half * RING + lax.axis_index("yc")

    whole = lambda *dims: pl.BlockSpec(dims, lambda i: (0,) * len(dims))

    table_send = pl.pallas_call(
        table_kernel,
        grid_spec=pltpu.PrefetchScalarGridSpec(
            num_scalar_prefetch=1,
            grid=(RING,),
            in_specs=[pl.BlockSpec((ROWS, WIDE), lambda i, place_ref: (0, place_ref[0] * RING + i))],
            out_specs=pl.BlockSpec((rows_x, 1, TILES * ROWS, L), lambda i, place_ref: (0, i, 0, 0)),
        ),
        out_shape=in_hbm(rows_x, RING, TILES * ROWS, L, BF16),
        compiler_params=PARAMS,
        name="table_send",
    )(half.reshape(1).astype(jnp.int32), value_table)
    table = exchange(table_send.reshape(OWNERS, TILES * ROWS, L), ("x", "yc"))

    batch_send, weights = pl.pallas_call(
        pack_kernel,
        grid=(GROUP,),
        in_specs=[
            whole(CANDS, TOK),
            whole(PICKS, TOK),
            whole(PICKS, TOK),
            pl.BlockSpec((TOK, WIDE), lambda i: (0, i)),
        ],
        out_specs=[pl.BlockSpec((1, WIDE + INFO, L), lambda i: (i, 0, 0)), whole(PICKS, TOK)],
        out_shape=(in_hbm(GROUP, WIDE + INFO, L, BF16), shape(PICKS, TOK, F32)),
        scratch_shapes=[pltpu.VMEM((INFO, TOK), BF16)],
        compiler_params=PARAMS,
        name="pack",
    )(owners.T, pick_index.T, key_scores.T, output_cotangent)
    batch = exchange(batch_send, ("dl", "yc"))
    gain = lax.dynamic_slice(norm_gain, (block_index * WIDE,), (WIDE,)).reshape(WIDE, 1)

    batch_spec = pl.BlockSpec((STEP, WIDE + INFO, L), lambda i: (i, 0, 0))
    table_spec = whole(OWNERS, TILES * ROWS, L)
    wide_spec = pl.BlockSpec((WIDE, STEP * TOK), lambda i: (0, i))
    sums_spec = pl.BlockSpec((GROUP, 2, STEP * TOK), lambda i: (0, 0, i))
    tokens = GROUP * TOK

    memory, sums_send = pl.pallas_call(
        forward_kernel,
        grid=(steps,),
        in_specs=[batch_spec, table_spec, whole(WIDE, 1)],
        out_specs=[wide_spec, sums_spec],
        out_shape=(shape(WIDE, tokens, F32), shape(GROUP, 2, tokens, F32)),
        scratch_shapes=[pltpu.VMEM((WIDE, TABLE), BF16)],
        compiler_params=PARAMS,
        name="forward",
    )(batch, table, gain)
    sums = exchange(sums_send, ("dl", "yc"))

    out_turned, memory_grad, grad_send = pl.pallas_call(
        backward_kernel,
        grid=(steps,),
        in_specs=[batch_spec, whole(WIDE, 1), wide_spec, sums_spec],
        out_specs=[wide_spec, wide_spec, whole(OWNERS, GRAD, L)],
        out_shape=(
            shape(WIDE, tokens, BF16),
            shape(WIDE, tokens, BF16),
            in_hbm(OWNERS, GRAD, L, BF16),
        ),
        scratch_shapes=[pltpu.VMEM((TABLE, WIDE), F32), pltpu.VMEM((WIDE, L), F32)],
        compiler_params=PARAMS,
        name="backward",
    )(batch, gain, memory, sums)
    plane_parts = exchange(grad_send, ("x", "yc"))

    back_send = pl.pallas_call(
        placed_grad_kernel,
        grid=(steps,),
        in_specs=[batch_spec, table_spec, wide_spec, wide_spec],
        out_specs=pl.BlockSpec((STEP, BACK, L), lambda i: (i, 0, 0)),
        out_shape=in_hbm(GROUP, BACK, L, BF16),
        compiler_params=PARAMS,
        name="placed_grad",
    )(batch, table, out_turned, memory_grad)

    shares_send = pl.pallas_call(
        plane_kernel,
        out_shape=in_hbm(RING, GRAD, L, BF16),
        compiler_params=PARAMS,
        name="plane_sum",
    )(plane_parts.reshape(rows_x, RING, GRAD, L))
    shares = exchange(shares_send, "dh")
    total_send = pl.pallas_call(
        share_kernel,
        out_shape=in_hbm(GROUP, GRAD, L, BF16),
        compiler_params=PARAMS,
        name="share_sum",
    )(shares)
    total = exchange(total_send, ("dl", "dh"))

    back = exchange(back_send, ("dl", "yc"))
    memory_out, score_turned = pl.pallas_call(
        out_kernel,
        grid=(GROUP,),
        in_specs=[pl.BlockSpec((1, BACK, L), lambda i: (i, 0, 0)), whole(PICKS, TOK), whole(PICKS, TOK)],
        out_specs=[pl.BlockSpec((TOK, WIDE), lambda i: (0, i)), whole(PICKS, TOK)],
        out_shape=(shape(TOK, D, BF16), shape(PICKS, TOK, F32)),
        scratch_shapes=[pltpu.VMEM((SLOTS, TOK), F32)],
        compiler_params=PARAMS,
        name="unpack",
    )(back, pick_index.T, weights)

    new_table, new_first, new_second, gain_gradient = pl.pallas_call(
        adam_kernel,
        out_shape=(
            shape(ROWS, D, BF16),
            shape(ROWS, D, F32),
            shape(ROWS, D, F32),
            shape(1, D, F32),
        ),
        compiler_params=PARAMS,
        name="adam",
    )(total, value_table, first_moment, second_moment)
    return (memory_out, score_turned.T, gain_gradient.reshape(D), new_table, new_first, new_second)


def solution(mesh):
    planes, mem_count = mesh.shape["dp"], mesh.shape["mem"]
    split_mesh = Mesh(
        mesh.devices.reshape(planes // PAIR, PAIR, mem_count // RING, RING), ("dh", "dl", "x", "yc")
    )
    tokens = P(("dh", "dl", "x", "yc"), None)
    rows = P(("x", "yc"), None)
    return jax.shard_map(
        per_device,
        mesh=split_mesh,
        in_specs=(tokens, tokens, tokens, tokens, rows, rows, rows, P()),
        out_specs=(tokens, tokens, P(), rows, rows, rows),
        check_vma=False,
    )
```

```python
import functools

import jax
import jax.numpy as jnp
from jax import lax
from jax.experimental import pallas as pl
from jax.experimental.pallas import tpu as pltpu
from jax.sharding import Mesh
from jax.sharding import PartitionSpec as P

beta_first = 0.9
beta_second = 0.95
learning_rate = 0.01
adam_epsilon = 1e-08
first_bias = 1.0 - (0.9**50) ** 2
second_bias = 1.0 - (0.95**50) ** 2
norm_epsilon = 1e-05

L = 128
PAIR = 2
RING = 8
GROUP = PAIR * RING
CANDS = 3
ROWS = 32
PICKS = 32
D = 4096
WIDE = D // GROUP
TILES = WIDE // L
TOK = 128
SLOTS = CANDS * ROWS
TABLE = 1024
OWNERS = TABLE // ROWS
INFO = SLOTS + 8
GAIN_AT = TILES * ROWS
GRAD = GAIN_AT + 8
BACK = WIDE + SLOTS
STEP = 4
MANY = 4
VMEM_LIMIT = 32 * 1024 * 1024
F32 = jnp.float32
BF16 = jnp.bfloat16
PARAMS = pltpu.CompilerParams(vmem_limit_bytes=VMEM_LIMIT)


def dot(a, b, dims):
    return lax.dot_general(a, b, (dims, ((), ())), preferred_element_type=F32)


def shape(*dims_and_type):
    return jax.ShapeDtypeStruct(dims_and_type[:-1], dims_and_type[-1])


def in_hbm(*dims_and_type):
    return pltpu.HBM(dims_and_type[:-1], dims_and_type[-1])


def table_kernel(place_ref, table_ref, out_ref):
    del place_ref
    for b in range(RING):
        for j in range(TILES):
            at = b * WIDE + j * L
            tile = table_ref[:, at : at + L]
            for x in range(out_ref.shape[0]):
                out_ref[x, b, j * ROWS : (j + 1) * ROWS, :] = tile


def pack_kernel(owners_ref, pick_ref, scores_ref, cotangent_ref, send_ref, weights_ref, info_ref):
    @pl.when(pl.program_id(0) == 0)
    def _():
        scores = scores_ref[...]
        shifted = jnp.exp(scores - jnp.max(scores, axis=0, keepdims=True))
        weights = shifted / jnp.sum(shifted, axis=0, keepdims=True)
        weights_ref[...] = weights
        pick = pick_ref[...]
        entry = lax.broadcasted_iota(jnp.int32, (SLOTS, TOK), 0)
        placed = jnp.zeros((SLOTS, TOK), F32)
        for k in range(PICKS):
            placed = jnp.where(pick[k : k + 1] == entry, weights[k : k + 1], placed)
        owners = owners_ref[...].astype(F32)
        line = lax.broadcasted_iota(jnp.int32, (8, TOK), 0)
        named = jnp.zeros((8, TOK), F32)
        for c in range(CANDS):
            named = jnp.where(line == c, owners[c : c + 1], named)
        info_ref[...] = jnp.concatenate([placed, named], axis=0).astype(BF16)

    for b in range(MANY):
        for j in range(TILES):
            at = b * WIDE + j * L
            send_ref[b, j * L : (j + 1) * L, :] = jnp.transpose(cotangent_ref[:, at : at + L])
        send_ref[b, WIDE:, :] = info_ref[...]


def load_info(batch_ref):
    info = jnp.concatenate([batch_ref[i, WIDE:, :] for i in range(STEP)], axis=1).astype(F32)
    placed = [info[c * ROWS : (c + 1) * ROWS] for c in range(CANDS)]
    named = [
        jnp.broadcast_to(info[SLOTS + c : SLOTS + c + 1], (ROWS, STEP * TOK)) for c in range(CANDS)
    ]
    return placed, named


def place(placed, named):
    blocks = []
    for o in range(OWNERS):
        block = jnp.zeros((ROWS, STEP * TOK), F32)
        for c in range(CANDS):
            block = jnp.where(named[c] == float(o), placed[c], block)
        blocks.append(block.astype(BF16))
    return jnp.concatenate(blocks, axis=0)


def load_table(table_ref):
    return jnp.concatenate(
        [table_ref[:, j * ROWS : (j + 1) * ROWS, :].reshape(TABLE, L) for j in range(TILES)], axis=1
    )


def load_cotangent(batch_ref):
    return jnp.concatenate([batch_ref[i, :WIDE, :] for i in range(STEP)], axis=1).astype(F32)


def forward_kernel(batch_ref, table_ref, gain_ref, memory_ref, sums_ref, turned_ref):
    @pl.when(pl.program_id(0) == 0)
    def _():
        turned_ref[...] = jnp.transpose(load_table(table_ref))

    memory = dot(turned_ref[...], place(*load_info(batch_ref)), ((1,), (0,)))
    memory_ref[...] = memory
    scaled = load_cotangent(batch_ref) * gain_ref[...]
    square = jnp.sum(memory * memory, axis=0, keepdims=True)
    cross = jnp.sum(scaled * memory, axis=0, keepdims=True)
    both = jnp.concatenate([square, cross], axis=0)
    for g in range(sums_ref.shape[0]):
        sums_ref[g] = both


def split(value):
    high = value.astype(BF16).astype(F32)
    return high, value - high


def gain_rows(rows):
    high, low = split(rows)
    return jnp.concatenate([high, low, jnp.zeros((8 - 2 * TILES, L), F32)], axis=0).astype(BF16)


def backward_kernel(batch_ref, gain_ref, memory_ref, sums_ref, out_ref, grad_ref, send_ref, total_ref, gain_sum_ref):
    step = pl.program_id(0)
    sums = jnp.sum(sums_ref[...], axis=0)
    inverse = lax.rsqrt(sums[0:1] / D + norm_epsilon)
    factor = inverse * inverse * inverse * (sums[1:2] / D)
    memory = memory_ref[...]
    cotangent = load_cotangent(batch_ref)
    gain = gain_ref[...]
    normed = memory * inverse
    out_ref[...] = (normed * gain).astype(BF16)
    grad = (inverse * (cotangent * gain) - memory * factor).astype(BF16)
    grad_ref[...] = grad
    gain_part = cotangent * normed
    folded = sum(gain_part[:, i * L : (i + 1) * L] for i in range(STEP))
    table_part = dot(place(*load_info(batch_ref)), grad, ((1,), (1,)))

    @pl.when(step == 0)
    def _():
        total_ref[...] = table_part
        gain_sum_ref[...] = folded

    @pl.when(step > 0)
    def _():
        total_ref[...] += table_part
        gain_sum_ref[...] += folded

    @pl.when(step == pl.num_programs(0) - 1)
    def _():
        for j in range(TILES):
            send_ref[:, j * ROWS : (j + 1) * ROWS, :] = (
                total_ref[:, j * L : (j + 1) * L].astype(BF16).reshape(OWNERS, ROWS, L)
            )
        turned = jnp.transpose(gain_sum_ref[...])
        rows = [jnp.sum(turned[:, j * L : (j + 1) * L], axis=0, keepdims=True) for j in range(TILES)]
        tail = gain_rows(jnp.concatenate(rows, axis=0))
        for o in range(OWNERS):
            send_ref[o, GAIN_AT:, :] = tail


def placed_grad_kernel(batch_ref, table_ref, out_ref, grad_ref, send_ref):
    _, named = load_info(batch_ref)
    full = dot(load_table(table_ref), grad_ref[...], ((1,), (0,)))
    found = [jnp.zeros((ROWS, STEP * TOK), F32) for _ in range(CANDS)]
    for o in range(OWNERS):
        block = full[o * ROWS : (o + 1) * ROWS]
        for c in range(CANDS):
            found[c] = jnp.where(named[c] == float(o), block, found[c])
    for i in range(STEP):
        send_ref[i, :WIDE, :] = out_ref[:, i * TOK : (i + 1) * TOK]
        for c in range(CANDS):
            send_ref[i, WIDE + c * ROWS : WIDE + (c + 1) * ROWS, :] = found[c][
                :, i * TOK : (i + 1) * TOK
            ].astype(BF16)


def merge(parts):
    total = jnp.sum(parts, axis=0)
    gain = total[GAIN_AT : GAIN_AT + TILES] + total[GAIN_AT + TILES : GAIN_AT + 2 * TILES]
    return total[:GAIN_AT], gain


def plane_kernel(parts_ref, send_ref):
    for b in range(parts_ref.shape[1]):
        rows, gain = merge(parts_ref[:, b].astype(F32))
        send_ref[b, :GAIN_AT, :] = rows.astype(BF16)
        send_ref[b, GAIN_AT:, :] = gain_rows(gain)


def share_kernel(parts_ref, send_ref):
    rows, gain = merge(parts_ref[...].astype(F32))
    send_ref[:GAIN_AT, :] = rows.astype(BF16)
    send_ref[GAIN_AT:, :] = gain_rows(gain)


def adam_kernel(grad_ref, table_ref, first_ref, second_ref, new_table_ref, new_first_ref, new_second_ref, gain_ref):
    for z in range(grad_ref.shape[0]):
        b = (z % PAIR) * RING + z // PAIR
        tail = grad_ref[z, GAIN_AT:, :].astype(F32)
        for j in range(TILES):
            at = b * WIDE + j * L
            grad = grad_ref[z, j * ROWS : (j + 1) * ROWS, :].astype(F32)
            first = beta_first * first_ref[:, at : at + L] + (1.0 - beta_first) * grad
            second = beta_second * second_ref[:, at : at + L] + (1.0 - beta_second) * grad * grad
            update = learning_rate * (first / first_bias) / (jnp.sqrt(second / second_bias) + adam_epsilon)
            new_first_ref[:, at : at + L] = first
            new_second_ref[:, at : at + L] = second
            new_table_ref[:, at : at + L] = (table_ref[:, at : at + L].astype(F32) - update).astype(BF16)
            gain_ref[:, at : at + L] = tail[j : j + 1] + tail[TILES + j : TILES + j + 1]


def out_kernel(parts_ref, pick_ref, weights_ref, out_ref, score_ref, placed_grad_ref):
    step = pl.program_id(0)
    for b in range(MANY):
        for j in range(TILES):
            at = b * WIDE + j * L
            out_ref[:, at : at + L] = jnp.transpose(parts_ref[b, j * L : (j + 1) * L, :])
    part = sum(parts_ref[b, WIDE:, :].astype(F32) for b in range(MANY))

    @pl.when(step == 0)
    def _():
        placed_grad_ref[...] = part

    @pl.when(step > 0)
    def _():
        placed_grad_ref[...] += part

    @pl.when(step == pl.num_programs(0) - 1)
    def _():
        pick = pick_ref[...]
        weights = weights_ref[...]
        weight_grad = jnp.zeros((PICKS, TOK), F32)
        for m in range(SLOTS):
            weight_grad = jnp.where(pick == m, placed_grad_ref[m : m + 1, :], weight_grad)
        mean = jnp.sum(weights * weight_grad, axis=0, keepdims=True)
        score_ref[...] = weights * (weight_grad - mean)


def exchange(array, axes):
    return lax.all_to_all(array, axes, split_axis=0, concat_axis=0, tiled=True)


def per_device(
    owners,
    pick_index,
    key_scores,
    output_cotangent,
    value_table,
    first_moment,
    second_moment,
    norm_gain,
):
    rows_x = lax.axis_size("x")
    steps = GROUP // STEP
    half = lax.axis_index("dl")
    block_index = half * RING + lax.axis_index("yc")

    whole = lambda *dims: pl.BlockSpec(dims, lambda i: (0,) * len(dims))

    table_send = pl.pallas_call(
        table_kernel,
        grid_spec=pltpu.PrefetchScalarGridSpec(
            num_scalar_prefetch=1,
            grid=(1,),
            in_specs=[pl.BlockSpec((ROWS, RING * WIDE), lambda i, place_ref: (0, place_ref[0]))],
            out_specs=pl.BlockSpec((rows_x, RING, TILES * ROWS, L), lambda i, place_ref: (0, 0, 0, 0)),
        ),
        out_shape=in_hbm(rows_x, RING, TILES * ROWS, L, BF16),
        compiler_params=PARAMS,
        name="table_send",
    )(half.reshape(1).astype(jnp.int32), value_table)
    table = exchange(table_send.reshape(OWNERS, TILES * ROWS, L), ("x", "yc"))

    batch_send, weights = pl.pallas_call(
        pack_kernel,
        grid=(GROUP // MANY,),
        in_specs=[
            whole(CANDS, TOK),
            whole(PICKS, TOK),
            whole(PICKS, TOK),
            pl.BlockSpec((TOK, MANY * WIDE), lambda i: (0, i)),
        ],
        out_specs=[pl.BlockSpec((MANY, WIDE + INFO, L), lambda i: (i, 0, 0)), whole(PICKS, TOK)],
        out_shape=(in_hbm(GROUP, WIDE + INFO, L, BF16), shape(PICKS, TOK, F32)),
        scratch_shapes=[pltpu.VMEM((INFO, TOK), BF16)],
        compiler_params=PARAMS,
        name="pack",
    )(owners.T, pick_index.T, key_scores.T, output_cotangent)
    batch = exchange(batch_send, ("dl", "yc"))
    gain = lax.dynamic_slice(norm_gain, (block_index * WIDE,), (WIDE,)).reshape(WIDE, 1)

    batch_spec = pl.BlockSpec((STEP, WIDE + INFO, L), lambda i: (i, 0, 0))
    table_spec = whole(OWNERS, TILES * ROWS, L)
    wide_spec = pl.BlockSpec((WIDE, STEP * TOK), lambda i: (0, i))
    sums_spec = pl.BlockSpec((GROUP, 2, STEP * TOK), lambda i: (0, 0, i))
    tokens = GROUP * TOK

    memory, sums_send = pl.pallas_call(
        forward_kernel,
        grid=(steps,),
        in_specs=[batch_spec, table_spec, whole(WIDE, 1)],
        out_specs=[wide_spec, sums_spec],
        out_shape=(shape(WIDE, tokens, F32), shape(GROUP, 2, tokens, F32)),
        scratch_shapes=[pltpu.VMEM((WIDE, TABLE), BF16)],
        compiler_params=PARAMS,
        name="forward",
    )(batch, table, gain)
    sums = exchange(sums_send, ("dl", "yc"))

    out_turned, memory_grad, grad_send = pl.pallas_call(
        backward_kernel,
        grid=(steps,),
        in_specs=[batch_spec, whole(WIDE, 1), wide_spec, sums_spec],
        out_specs=[wide_spec, wide_spec, whole(OWNERS, GRAD, L)],
        out_shape=(
            in_hbm(WIDE, tokens, BF16),
            in_hbm(WIDE, tokens, BF16),
            in_hbm(OWNERS, GRAD, L, BF16),
        ),
        scratch_shapes=[pltpu.VMEM((TABLE, WIDE), F32), pltpu.VMEM((WIDE, L), F32)],
        compiler_params=PARAMS,
        name="backward",
    )(batch, gain, memory, sums)
    plane_parts = exchange(grad_send, ("x", "yc"))

    back_send = pl.pallas_call(
        placed_grad_kernel,
        grid=(steps,),
        in_specs=[batch_spec, table_spec, wide_spec, wide_spec],
        out_specs=pl.BlockSpec((STEP, BACK, L), lambda i: (i, 0, 0)),
        out_shape=in_hbm(GROUP, BACK, L, BF16),
        compiler_params=PARAMS,
        name="placed_grad",
    )(batch, table, out_turned, memory_grad)

    plane_parts, back_send = lax.optimization_barrier((plane_parts, back_send))
    shares_send = pl.pallas_call(
        plane_kernel,
        out_shape=shape(RING, GRAD, L, BF16),
        compiler_params=PARAMS,
        name="plane_sum",
    )(plane_parts.reshape(rows_x, RING, GRAD, L))
    shares = exchange(shares_send, "dh")
    total = pl.pallas_call(
        share_kernel,
        out_shape=shape(GRAD, L, BF16),
        compiler_params=PARAMS,
        name="share_sum",
    )(shares)
    total, back_send = lax.optimization_barrier((total, back_send))
    totals = lax.all_gather(total, ("dh", "dl"), axis=0, tiled=False)

    back = exchange(back_send, ("dl", "yc"))
    memory_out, score_turned = pl.pallas_call(
        out_kernel,
        grid=(GROUP // MANY,),
        in_specs=[pl.BlockSpec((MANY, BACK, L), lambda i: (i, 0, 0)), whole(PICKS, TOK), whole(PICKS, TOK)],
        out_specs=[pl.BlockSpec((TOK, MANY * WIDE), lambda i: (0, i)), whole(PICKS, TOK)],
        out_shape=(shape(TOK, D, BF16), shape(PICKS, TOK, F32)),
        scratch_shapes=[pltpu.VMEM((SLOTS, TOK), F32)],
        compiler_params=PARAMS,
        name="unpack",
    )(back, pick_index.T, weights)

    new_table, new_first, new_second, gain_gradient = pl.pallas_call(
        adam_kernel,
        out_shape=(
            shape(ROWS, D, BF16),
            shape(ROWS, D, F32),
            shape(ROWS, D, F32),
            shape(1, D, F32),
        ),
        compiler_params=PARAMS,
        name="adam",
    )(totals, value_table, first_moment, second_moment)
    return (memory_out, score_turned.T, gain_gradient.reshape(D), new_table, new_first, new_second)


def solution(mesh):
    planes, mem_count = mesh.shape["dp"], mesh.shape["mem"]
    split_mesh = Mesh(
        mesh.devices.reshape(planes // PAIR, PAIR, mem_count // RING, RING), ("dh", "dl", "x", "yc")
    )
    tokens = P(("dh", "dl", "x", "yc"), None)
    rows = P(("x", "yc"), None)
    return jax.shard_map(
        per_device,
        mesh=split_mesh,
        in_specs=(tokens, tokens, tokens, tokens, rows, rows, rows, P()),
        out_specs=(tokens, tokens, P(), rows, rows, rows),
        check_vma=False,
    )
```

```python
import functools

import jax
import jax.numpy as jnp
from jax import lax
from jax.experimental import pallas as pl
from jax.experimental.pallas import tpu as pltpu
from jax.sharding import Mesh
from jax.sharding import PartitionSpec as P

beta_first = 0.9
beta_second = 0.95
learning_rate = 0.01
adam_epsilon = 1e-08
first_bias = 1.0 - (0.9**50) ** 2
second_bias = 1.0 - (0.95**50) ** 2
norm_epsilon = 1e-05

L = 128
PAIR = 2
RING = 8
GROUP = PAIR * RING
CHIPS = GROUP // 2
CANDS = 3
ROWS = 32
PICKS = 32
D = 4096
WIDE = D // GROUP
TILES = WIDE // L
TOK = 128
SLOTS = CANDS * ROWS
TABLE = 1024
OWNERS = TABLE // ROWS
INFO = SLOTS + 8
GAIN_AT = TILES * ROWS
GRAD = GAIN_AT + 8
BACK = WIDE + SLOTS
STEP = 4
MANY = 4
VMEM_LIMIT = 32 * 1024 * 1024
F32 = jnp.float32
BF16 = jnp.bfloat16
PARAMS = pltpu.CompilerParams(vmem_limit_bytes=VMEM_LIMIT)


def dot(a, b, dims):
    return lax.dot_general(a, b, (dims, ((), ())), preferred_element_type=F32)


def shape(*dims_and_type):
    return jax.ShapeDtypeStruct(dims_and_type[:-1], dims_and_type[-1])


def in_hbm(*dims_and_type):
    return pltpu.HBM(dims_and_type[:-1], dims_and_type[-1])


def table_kernel(place_ref, table_ref, out_ref):
    del place_ref
    for b in range(RING):
        for j in range(TILES):
            at = b * WIDE + j * L
            tile = table_ref[:, at : at + L]
            for x in range(out_ref.shape[0]):
                out_ref[x, b, j * ROWS : (j + 1) * ROWS, :] = tile


def pack_kernel(owners_ref, pick_ref, scores_ref, cotangent_ref, send_ref, weights_ref, info_ref):
    @pl.when(pl.program_id(0) == 0)
    def _():
        scores = scores_ref[...]
        shifted = jnp.exp(scores - jnp.max(scores, axis=0, keepdims=True))
        weights = shifted / jnp.sum(shifted, axis=0, keepdims=True)
        weights_ref[...] = weights
        pick = pick_ref[...]
        entry = lax.broadcasted_iota(jnp.int32, (SLOTS, TOK), 0)
        placed = jnp.zeros((SLOTS, TOK), F32)
        for k in range(PICKS):
            placed = jnp.where(pick[k : k + 1] == entry, weights[k : k + 1], placed)
        owners = owners_ref[...].astype(F32)
        line = lax.broadcasted_iota(jnp.int32, (8, TOK), 0)
        named = jnp.zeros((8, TOK), F32)
        for c in range(CANDS):
            named = jnp.where(line == c, owners[c : c + 1], named)
        info_ref[...] = jnp.concatenate([placed, named], axis=0).astype(BF16)

    for b in range(MANY):
        for j in range(TILES):
            at = b * WIDE + j * L
            send_ref[b, j * L : (j + 1) * L, :] = jnp.transpose(cotangent_ref[:, at : at + L])
        send_ref[b, WIDE:, :] = info_ref[...]


def load_info(batch_ref):
    info = jnp.concatenate([batch_ref[i, WIDE:, :] for i in range(STEP)], axis=1).astype(F32)
    placed = [info[c * ROWS : (c + 1) * ROWS] for c in range(CANDS)]
    named = [
        jnp.broadcast_to(info[SLOTS + c : SLOTS + c + 1], (ROWS, STEP * TOK)) for c in range(CANDS)
    ]
    return placed, named


def place(placed, named):
    blocks = []
    for o in range(OWNERS):
        block = jnp.zeros((ROWS, STEP * TOK), F32)
        for c in range(CANDS):
            block = jnp.where(named[c] == float(o), placed[c], block)
        blocks.append(block.astype(BF16))
    return jnp.concatenate(blocks, axis=0)


def load_table(table_ref):
    return jnp.concatenate(
        [table_ref[:, j * ROWS : (j + 1) * ROWS, :].reshape(TABLE, L) for j in range(TILES)], axis=1
    )


def load_cotangent(batch_ref):
    return jnp.concatenate([batch_ref[i, :WIDE, :] for i in range(STEP)], axis=1).astype(F32)


def forward_kernel(batch_ref, table_ref, gain_ref, memory_ref, sums_ref, turned_ref):
    @pl.when(pl.program_id(0) == 0)
    def _():
        turned_ref[...] = jnp.transpose(load_table(table_ref))

    memory = dot(turned_ref[...], place(*load_info(batch_ref)), ((1,), (0,)))
    memory_ref[...] = memory
    scaled = load_cotangent(batch_ref) * gain_ref[...]
    square = jnp.sum(memory * memory, axis=0, keepdims=True)
    cross = jnp.sum(scaled * memory, axis=0, keepdims=True)
    both = jnp.concatenate([square, cross], axis=0)
    for g in range(sums_ref.shape[0]):
        sums_ref[g] = both


def split(value):
    high = value.astype(BF16).astype(F32)
    return high, value - high


def gain_rows(rows):
    high, low = split(rows)
    return jnp.concatenate([high, low, jnp.zeros((8 - 2 * TILES, L), F32)], axis=0).astype(BF16)


def backward_kernel(batch_ref, gain_ref, memory_ref, sums_ref, out_ref, grad_ref, send_ref, total_ref, gain_sum_ref):
    step = pl.program_id(0)
    sums = jnp.sum(sums_ref[...], axis=0)
    inverse = lax.rsqrt(sums[0:1] / D + norm_epsilon)
    factor = inverse * inverse * inverse * (sums[1:2] / D)
    memory = memory_ref[...]
    cotangent = load_cotangent(batch_ref)
    gain = gain_ref[...]
    normed = memory * inverse
    out_ref[...] = (normed * gain).astype(BF16)
    grad = (inverse * (cotangent * gain) - memory * factor).astype(BF16)
    grad_ref[...] = grad
    gain_part = cotangent * normed
    folded = sum(gain_part[:, i * L : (i + 1) * L] for i in range(STEP))
    table_part = dot(place(*load_info(batch_ref)), grad, ((1,), (1,)))

    @pl.when(step == 0)
    def _():
        total_ref[...] = table_part
        gain_sum_ref[...] = folded

    @pl.when(step > 0)
    def _():
        total_ref[...] += table_part
        gain_sum_ref[...] += folded

    @pl.when(step == pl.num_programs(0) - 1)
    def _():
        for j in range(TILES):
            send_ref[:, j * ROWS : (j + 1) * ROWS, :] = (
                total_ref[:, j * L : (j + 1) * L].astype(BF16).reshape(OWNERS, ROWS, L)
            )
        turned = jnp.transpose(gain_sum_ref[...])
        rows = [jnp.sum(turned[:, j * L : (j + 1) * L], axis=0, keepdims=True) for j in range(TILES)]
        tail = gain_rows(jnp.concatenate(rows, axis=0))
        for o in range(OWNERS):
            send_ref[o, GAIN_AT:, :] = tail


def placed_grad_kernel(place_ref, batch_ref, table_ref, out_ref, grad_ref, same_ref, other_ref, stage_ref):
    _, named = load_info(batch_ref)
    full = dot(load_table(table_ref), grad_ref[...], ((1,), (0,)))
    found = [jnp.zeros((ROWS, STEP * TOK), F32) for _ in range(CANDS)]
    for o in range(OWNERS):
        block = full[o * ROWS : (o + 1) * ROWS]
        for c in range(CANDS):
            found[c] = jnp.where(named[c] == float(o), block, found[c])
    stage_ref[:WIDE, :] = out_ref[...]
    for c in range(CANDS):
        stage_ref[WIDE + c * ROWS : WIDE + (c + 1) * ROWS, :] = found[c].astype(BF16)
    low = lax.rem(place_ref[0], STEP)
    for s in range(GROUP // STEP):

        @pl.when(pl.program_id(0) == s)
        def _():
            for u in range(STEP):
                at = pl.multiple_of(lax.bitwise_xor(low, u) * TOK, TOK)
                send_ref = other_ref if u % 2 else same_ref
                send_ref[(s * STEP + u) // 2] = stage_ref[:, pl.ds(at, TOK)]


def merge_kernel(same_ref, other_ref, *send_refs):
    for k, send_ref in enumerate(send_refs):
        send_ref[:WIDE, :] = same_ref[k, :WIDE, :]
        send_ref[WIDE : 2 * WIDE, :] = other_ref[k, :WIDE, :]
        both = same_ref[k, WIDE:, :].astype(F32) + other_ref[k, WIDE:, :].astype(F32)
        send_ref[2 * WIDE :, :] = both.astype(BF16)


def merge(parts):
    total = jnp.sum(parts, axis=0)
    gain = total[GAIN_AT : GAIN_AT + TILES] + total[GAIN_AT + TILES : GAIN_AT + 2 * TILES]
    return total[:GAIN_AT], gain


def plane_kernel(parts_ref, send_ref):
    for b in range(parts_ref.shape[1]):
        rows, gain = merge(parts_ref[:, b].astype(F32))
        send_ref[b, :GAIN_AT, :] = rows.astype(BF16)
        send_ref[b, GAIN_AT:, :] = gain_rows(gain)


def share_kernel(parts_ref, send_ref):
    rows, gain = merge(parts_ref[...].astype(F32))
    rows = rows.astype(BF16)
    tail = gain_rows(gain)
    for b in range(send_ref.shape[0]):
        send_ref[b, :GAIN_AT, :] = rows
        send_ref[b, GAIN_AT:, :] = tail


def adam_kernel(grad_ref, table_ref, first_ref, second_ref, new_table_ref, new_first_ref, new_second_ref, gain_ref):
    for b in range(grad_ref.shape[0]):
        tail = grad_ref[b, GAIN_AT:, :].astype(F32)
        for j in range(TILES):
            at = b * WIDE + j * L
            grad = grad_ref[b, j * ROWS : (j + 1) * ROWS, :].astype(F32)
            first = beta_first * first_ref[:, at : at + L] + (1.0 - beta_first) * grad
            second = beta_second * second_ref[:, at : at + L] + (1.0 - beta_second) * grad * grad
            update = learning_rate * (first / first_bias) / (jnp.sqrt(second / second_bias) + adam_epsilon)
            new_first_ref[:, at : at + L] = first
            new_second_ref[:, at : at + L] = second
            new_table_ref[:, at : at + L] = (table_ref[:, at : at + L].astype(F32) - update).astype(BF16)
            gain_ref[:, at : at + L] = tail[j : j + 1] + tail[TILES + j : TILES + j + 1]


def out_kernel(place_ref, pick_ref, weights_ref, *refs):
    parts, (out_ref, score_ref, placed_grad_ref) = refs[:-3], refs[-3:]
    for k, part_ref in enumerate(parts):
        for core in range(2):
            start = lax.bitwise_xor(place_ref[0], 2 * k + core) * WIDE
            for j in range(TILES):
                at = pl.multiple_of(start + j * L, L)
                row = core * WIDE + j * L
                out_ref[:, pl.ds(at, L)] = jnp.transpose(part_ref[row : row + L, :])
    placed_grad_ref[...] = sum(part_ref[2 * WIDE :, :].astype(F32) for part_ref in parts)
    pick = pick_ref[...]
    weights = weights_ref[...]
    weight_grad = jnp.zeros((PICKS, TOK), F32)
    for m in range(SLOTS):
        weight_grad = jnp.where(pick == m, placed_grad_ref[m : m + 1, :], weight_grad)
    mean = jnp.sum(weights * weight_grad, axis=0, keepdims=True)
    score_ref[...] = weights * (weight_grad - mean)


def exchange(array, axes):
    return lax.all_to_all(array, axes, split_axis=0, concat_axis=0, tiled=True)


def swap(array, k):
    return lax.ppermute(array, ("dl", "yc"), [(i, i ^ k) for i in range(GROUP)])


def per_device(
    owners,
    pick_index,
    key_scores,
    output_cotangent,
    value_table,
    first_moment,
    second_moment,
    norm_gain,
):
    rows_x = lax.axis_size("x")
    steps = GROUP // STEP
    half = lax.axis_index("dl")
    block_index = half * RING + lax.axis_index("yc")

    whole = lambda *dims: pl.BlockSpec(dims, lambda i: (0,) * len(dims))

    table_send = pl.pallas_call(
        table_kernel,
        grid_spec=pltpu.PrefetchScalarGridSpec(
            num_scalar_prefetch=1,
            grid=(1,),
            in_specs=[pl.BlockSpec((ROWS, RING * WIDE), lambda i, place_ref: (0, place_ref[0]))],
            out_specs=pl.BlockSpec((rows_x, RING, TILES * ROWS, L), lambda i, place_ref: (0, 0, 0, 0)),
        ),
        out_shape=in_hbm(rows_x, RING, TILES * ROWS, L, BF16),
        compiler_params=PARAMS,
        name="table_send",
    )(half.reshape(1).astype(jnp.int32), value_table)
    table = exchange(table_send.reshape(OWNERS, TILES * ROWS, L), ("x", "yc"))

    batch_send, weights = pl.pallas_call(
        pack_kernel,
        grid=(GROUP // MANY,),
        in_specs=[
            whole(CANDS, TOK),
            whole(PICKS, TOK),
            whole(PICKS, TOK),
            pl.BlockSpec((TOK, MANY * WIDE), lambda i: (0, i)),
        ],
        out_specs=[pl.BlockSpec((MANY, WIDE + INFO, L), lambda i: (i, 0, 0)), whole(PICKS, TOK)],
        out_shape=(in_hbm(GROUP, WIDE + INFO, L, BF16), shape(PICKS, TOK, F32)),
        scratch_shapes=[pltpu.VMEM((INFO, TOK), BF16)],
        compiler_params=PARAMS,
        name="pack",
    )(owners.T, pick_index.T, key_scores.T, output_cotangent)
    batch = exchange(batch_send, ("dl", "yc"))
    gain = lax.dynamic_slice(norm_gain, (block_index * WIDE,), (WIDE,)).reshape(WIDE, 1)

    batch_spec = pl.BlockSpec((STEP, WIDE + INFO, L), lambda i: (i, 0, 0))
    table_spec = whole(OWNERS, TILES * ROWS, L)
    wide_spec = pl.BlockSpec((WIDE, STEP * TOK), lambda i: (0, i))
    sums_spec = pl.BlockSpec((GROUP, 2, STEP * TOK), lambda i: (0, 0, i))
    tokens = GROUP * TOK

    memory, sums_send = pl.pallas_call(
        forward_kernel,
        grid=(steps,),
        in_specs=[batch_spec, table_spec, whole(WIDE, 1)],
        out_specs=[wide_spec, sums_spec],
        out_shape=(shape(WIDE, tokens, F32), shape(GROUP, 2, tokens, F32)),
        scratch_shapes=[pltpu.VMEM((WIDE, TABLE), BF16)],
        compiler_params=PARAMS,
        name="forward",
    )(batch, table, gain)
    sums = exchange(sums_send, ("dl", "yc"))

    out_turned, memory_grad, grad_send = pl.pallas_call(
        backward_kernel,
        grid=(steps,),
        in_specs=[batch_spec, whole(WIDE, 1), wide_spec, sums_spec],
        out_specs=[wide_spec, wide_spec, whole(OWNERS, GRAD, L)],
        out_shape=(
            in_hbm(WIDE, tokens, BF16),
            in_hbm(WIDE, tokens, BF16),
            in_hbm(OWNERS, GRAD, L, BF16),
        ),
        scratch_shapes=[pltpu.VMEM((TABLE, WIDE), F32), pltpu.VMEM((WIDE, L), F32)],
        compiler_params=PARAMS,
        name="backward",
    )(batch, gain, memory, sums)
    plane_parts = exchange(grad_send, ("x", "yc"))

    place_in_group = block_index.reshape(1).astype(jnp.int32)
    turn = lambda i, place_ref: lax.bitwise_xor(i, lax.div(place_ref[0], STEP))
    same, other = pl.pallas_call(
        placed_grad_kernel,
        grid_spec=pltpu.PrefetchScalarGridSpec(
            num_scalar_prefetch=1,
            grid=(steps,),
            in_specs=[
                pl.BlockSpec((STEP, WIDE + INFO, L), lambda i, place_ref: (turn(i, place_ref), 0, 0)),
                pl.BlockSpec((OWNERS, TILES * ROWS, L), lambda i, place_ref: (0, 0, 0)),
                pl.BlockSpec((WIDE, STEP * TOK), lambda i, place_ref: (0, turn(i, place_ref))),
                pl.BlockSpec((WIDE, STEP * TOK), lambda i, place_ref: (0, turn(i, place_ref))),
            ],
            out_specs=[pl.BlockSpec((CHIPS, BACK, L), lambda i, place_ref: (0, 0, 0))] * 2,
            scratch_shapes=[pltpu.VMEM((BACK, STEP * TOK), BF16)],
        ),
        out_shape=[shape(CHIPS, BACK, L, BF16)] * 2,
        compiler_params=PARAMS,
        name="placed_grad",
    )(place_in_group, batch, table, out_turned, memory_grad)
    other = swap(other, 1)
    back_send = pl.pallas_call(
        merge_kernel,
        out_shape=[shape(2 * WIDE + SLOTS, L, BF16)] * CHIPS,
        compiler_params=PARAMS,
        name="merge",
    )(same, other)

    plane_parts, back_send = lax.optimization_barrier((plane_parts, back_send))
    shares_send = pl.pallas_call(
        plane_kernel,
        out_shape=shape(RING, GRAD, L, BF16),
        compiler_params=PARAMS,
        name="plane_sum",
    )(plane_parts.reshape(rows_x, RING, GRAD, L))
    shares_send, back_send = lax.optimization_barrier((shares_send, back_send))
    shares = exchange(shares_send, "dh")
    half_way = CHIPS // 2
    back = [swap(back_send[k], 2 * k) for k in range(1, half_way)]
    shares, back = lax.optimization_barrier((shares, back))
    total_send = pl.pallas_call(
        share_kernel,
        out_shape=shape(GROUP, GRAD, L, BF16),
        compiler_params=PARAMS,
        name="share_sum",
    )(shares)
    total_send, late_send = lax.optimization_barrier((total_send, back_send[half_way:]))
    total = exchange(total_send, ("dl", "dh"))
    late = [swap(late_send[k - half_way], 2 * k) for k in range(half_way, CHIPS)]
    total, late = lax.optimization_barrier((total, late))

    vmem = pl.BlockSpec(memory_space=pltpu.VMEM)
    smem = pl.BlockSpec(memory_space=pltpu.SMEM)
    memory_out, score_turned = pl.pallas_call(
        out_kernel,
        in_specs=[smem] + [vmem] * (2 + CHIPS),
        out_specs=[vmem, vmem],
        out_shape=(shape(TOK, D, BF16), shape(PICKS, TOK, F32)),
        scratch_shapes=[pltpu.VMEM((SLOTS, TOK), F32)],
        compiler_params=PARAMS,
        name="unpack",
    )(place_in_group, pick_index.T, weights, back_send[0], *back, *late)

    new_table, new_first, new_second, gain_gradient = pl.pallas_call(
        adam_kernel,
        out_shape=(
            shape(ROWS, D, BF16),
            shape(ROWS, D, F32),
            shape(ROWS, D, F32),
            shape(1, D, F32),
        ),
        compiler_params=PARAMS,
        name="adam",
    )(total, value_table, first_moment, second_moment)
    return (memory_out, score_turned.T, gain_gradient.reshape(D), new_table, new_first, new_second)


def solution(mesh):
    planes, mem_count = mesh.shape["dp"], mesh.shape["mem"]
    split_mesh = Mesh(
        mesh.devices.reshape(planes // PAIR, PAIR, mem_count // RING, RING), ("dh", "dl", "x", "yc")
    )
    tokens = P(("dh", "dl", "x", "yc"), None)
    rows = P(("x", "yc"), None)
    return jax.shard_map(
        per_device,
        mesh=split_mesh,
        in_specs=(tokens, tokens, tokens, tokens, rows, rows, rows, P()),
        out_specs=(tokens, tokens, P(), rows, rows, rows),
        check_vma=False,
    )
```

```python
import functools

import jax
import jax.numpy as jnp
from jax import lax
from jax.experimental import pallas as pl
from jax.experimental.pallas import tpu as pltpu
from jax.sharding import Mesh
from jax.sharding import PartitionSpec as P

beta_first = 0.9
beta_second = 0.95
learning_rate = 0.01
adam_epsilon = 1e-08
first_bias = 1.0 - (0.9**50) ** 2
second_bias = 1.0 - (0.95**50) ** 2
norm_epsilon = 1e-05

L = 128
PAIR = 2
RING = 8
GROUP = PAIR * RING
CANDS = 3
ROWS = 32
PICKS = 32
D = 4096
WIDE = D // GROUP
TILES = WIDE // L
TOK = 128
SLOTS = CANDS * ROWS
TABLE = 1024
OWNERS = TABLE // ROWS
INFO = SLOTS + 8
GAIN_AT = TILES * ROWS
GRAD = GAIN_AT + 8
BACK = WIDE + SLOTS
STEP = 4
MANY = 4
VMEM_LIMIT = 32 * 1024 * 1024
F32 = jnp.float32
BF16 = jnp.bfloat16
PARAMS = pltpu.CompilerParams(vmem_limit_bytes=VMEM_LIMIT)


def dot(a, b, dims):
    return lax.dot_general(a, b, (dims, ((), ())), preferred_element_type=F32)


def shape(*dims_and_type):
    return jax.ShapeDtypeStruct(dims_and_type[:-1], dims_and_type[-1])


def in_hbm(*dims_and_type):
    return pltpu.HBM(dims_and_type[:-1], dims_and_type[-1])


def table_core_kernel(place_ref, table_ref, same_ref, other_ref):
    for k in range(RING // 2):
        for core, out_ref in enumerate((same_ref, other_ref)):
            block = lax.bitwise_xor(place_ref[2], k) * 2 + lax.bitwise_xor(place_ref[3], core)
            for j in range(TILES):
                at = pl.multiple_of(block * WIDE + j * L, L)
                out_ref[k, j * ROWS : (j + 1) * ROWS, :] = table_ref[:, pl.ds(at, L)]


def table_y_kernel(place_ref, same_ref, got_ref, *send_refs):
    for k, send_ref in enumerate(send_refs):
        send_ref[place_ref[3]] = same_ref[k]
        send_ref[1 - place_ref[3]] = got_ref[k]


def table_join_kernel(axis, place_ref, *refs):
    out_ref = refs[-1]
    for k, part_ref in enumerate(refs[:-1]):
        out_ref[lax.bitwise_xor(place_ref[axis], k)] = part_ref[...]


def pack_kernel(owners_ref, pick_ref, scores_ref, cotangent_ref, send_ref, weights_ref, info_ref):
    @pl.when(pl.program_id(0) == 0)
    def _():
        scores = scores_ref[...]
        shifted = jnp.exp(scores - jnp.max(scores, axis=0, keepdims=True))
        weights = shifted / jnp.sum(shifted, axis=0, keepdims=True)
        weights_ref[...] = weights
        pick = pick_ref[...]
        entry = lax.broadcasted_iota(jnp.int32, (SLOTS, TOK), 0)
        placed = jnp.zeros((SLOTS, TOK), F32)
        for k in range(PICKS):
            placed = jnp.where(pick[k : k + 1] == entry, weights[k : k + 1], placed)
        owners = owners_ref[...].astype(F32)
        line = lax.broadcasted_iota(jnp.int32, (8, TOK), 0)
        named = jnp.zeros((8, TOK), F32)
        for c in range(CANDS):
            named = jnp.where(line == c, owners[c : c + 1], named)
        info_ref[...] = jnp.concatenate([placed, named], axis=0).astype(BF16)

    for b in range(MANY):
        for j in range(TILES):
            at = b * WIDE + j * L
            send_ref[b, j * L : (j + 1) * L, :] = jnp.transpose(cotangent_ref[:, at : at + L])
        send_ref[b, WIDE:, :] = info_ref[...]


def load_info(batch_ref):
    info = jnp.concatenate([batch_ref[i, WIDE:, :] for i in range(STEP)], axis=1).astype(F32)
    placed = [info[c * ROWS : (c + 1) * ROWS] for c in range(CANDS)]
    named = [
        jnp.broadcast_to(info[SLOTS + c : SLOTS + c + 1], (ROWS, STEP * TOK)) for c in range(CANDS)
    ]
    return placed, named


def place(placed, named):
    blocks = []
    for o in range(OWNERS):
        block = jnp.zeros((ROWS, STEP * TOK), F32)
        for c in range(CANDS):
            block = jnp.where(named[c] == float(o), placed[c], block)
        blocks.append(block.astype(BF16))
    return jnp.concatenate(blocks, axis=0)


def load_table(table_ref):
    return jnp.concatenate(
        [table_ref[:, j * ROWS : (j + 1) * ROWS, :].reshape(TABLE, L) for j in range(TILES)], axis=1
    )


def load_cotangent(batch_ref):
    return jnp.concatenate([batch_ref[i, :WIDE, :] for i in range(STEP)], axis=1).astype(F32)


def forward_kernel(batch_ref, table_ref, gain_ref, memory_ref, sums_ref, turned_ref):
    @pl.when(pl.program_id(0) == 0)
    def _():
        turned_ref[...] = jnp.transpose(load_table(table_ref))

    memory = dot(turned_ref[...], place(*load_info(batch_ref)), ((1,), (0,)))
    memory_ref[...] = memory
    scaled = load_cotangent(batch_ref) * gain_ref[...]
    square = jnp.sum(memory * memory, axis=0, keepdims=True)
    cross = jnp.sum(scaled * memory, axis=0, keepdims=True)
    both = jnp.concatenate([square, cross], axis=0)
    for g in range(sums_ref.shape[0]):
        sums_ref[g] = both


def split(value):
    high = value.astype(BF16).astype(F32)
    return high, value - high


def gain_rows(rows):
    high, low = split(rows)
    return jnp.concatenate([high, low, jnp.zeros((8 - 2 * TILES, L), F32)], axis=0).astype(BF16)


def backward_kernel(place_ref, batch_ref, gain_ref, memory_ref, sums_ref, out_ref, grad_ref, *refs):
    send_refs, (total_ref, gain_sum_ref) = refs[:-2], refs[-2:]
    step = pl.program_id(0)
    sums = jnp.sum(sums_ref[...], axis=0)
    inverse = lax.rsqrt(sums[0:1] / D + norm_epsilon)
    factor = inverse * inverse * inverse * (sums[1:2] / D)
    memory = memory_ref[...]
    cotangent = load_cotangent(batch_ref)
    gain = gain_ref[...]
    normed = memory * inverse
    out_ref[...] = (normed * gain).astype(BF16)
    grad = (inverse * (cotangent * gain) - memory * factor).astype(BF16)
    grad_ref[...] = grad
    gain_part = cotangent * normed
    folded = sum(gain_part[:, i * L : (i + 1) * L] for i in range(STEP))
    table_part = dot(place(*load_info(batch_ref)), grad, ((1,), (1,)))

    @pl.when(step == 0)
    def _():
        total_ref[...] = table_part
        gain_sum_ref[...] = folded

    @pl.when(step > 0)
    def _():
        total_ref[...] += table_part
        gain_sum_ref[...] += folded

    @pl.when(step == pl.num_programs(0) - 1)
    def _():
        turned = jnp.transpose(gain_sum_ref[...])
        rows = [jnp.sum(turned[:, j * L : (j + 1) * L], axis=0, keepdims=True) for j in range(TILES)]
        tail = gain_rows(jnp.concatenate(rows, axis=0))
        for k, send_ref in enumerate(send_refs):
            start = pl.multiple_of(lax.bitwise_xor(place_ref[1], k) * RING * ROWS, RING * ROWS)
            part = total_ref[pl.ds(start, RING * ROWS), :].astype(BF16)
            for o in range(RING):
                for j in range(TILES):
                    at = o * GAIN_AT + j * ROWS
                    send_ref[at : at + ROWS, :] = part[o * ROWS : (o + 1) * ROWS, j * L : (j + 1) * L]
            send_ref[RING * GAIN_AT :, :] = tail


def placed_grad_kernel(batch_ref, table_ref, out_ref, grad_ref, send_ref):
    _, named = load_info(batch_ref)
    full = dot(load_table(table_ref), grad_ref[...], ((1,), (0,)))
    found = [jnp.zeros((ROWS, STEP * TOK), F32) for _ in range(CANDS)]
    for o in range(OWNERS):
        block = full[o * ROWS : (o + 1) * ROWS]
        for c in range(CANDS):
            found[c] = jnp.where(named[c] == float(o), block, found[c])
    for i in range(STEP):
        send_ref[i, :WIDE, :] = out_ref[:, i * TOK : (i + 1) * TOK]
        for c in range(CANDS):
            send_ref[i, WIDE + c * ROWS : WIDE + (c + 1) * ROWS, :] = found[c][
                :, i * TOK : (i + 1) * TOK
            ].astype(BF16)


def merge(parts):
    total = jnp.sum(parts, axis=0)
    gain = total[GAIN_AT : GAIN_AT + TILES] + total[GAIN_AT + TILES : GAIN_AT + 2 * TILES]
    return total[:GAIN_AT], gain


def x_sum_kernel(place_ref, *refs):
    parts, send_refs = refs[: len(refs) // 2], refs[len(refs) // 2 :]
    last = sum(part_ref[RING * GAIN_AT :, :].astype(F32) for part_ref in parts)
    tail = gain_rows(last[:TILES] + last[TILES : 2 * TILES])
    for k, send_ref in enumerate(send_refs):
        at = pl.ds(pl.multiple_of(lax.bitwise_xor(place_ref[2], k) * 2 * GAIN_AT, 2 * GAIN_AT), 2 * GAIN_AT)
        send_ref[: 2 * GAIN_AT, :] = sum(part_ref[at, :].astype(F32) for part_ref in parts).astype(BF16)
        send_ref[2 * GAIN_AT :, :] = tail


def y_join_kernel(place_ref, *refs):
    parts, (same_ref, other_ref) = refs[:-2], refs[-2:]
    for k, part_ref in enumerate(parts):
        for core, out_ref in enumerate((same_ref, other_ref)):
            start = pl.multiple_of(lax.bitwise_xor(place_ref[3], core) * GAIN_AT, GAIN_AT)
            out_ref[k, :GAIN_AT, :] = part_ref[pl.ds(start, GAIN_AT), :]
            out_ref[k, GAIN_AT:, :] = part_ref[2 * GAIN_AT :, :]


def plane_kernel(place_ref, same_ref, got_ref, send_ref):
    for k in range(RING // 2):
        for core, part_ref in enumerate((same_ref, got_ref)):
            block = lax.bitwise_xor(place_ref[2], k) * 2 + lax.bitwise_xor(place_ref[3], core)
            send_ref[block] = part_ref[k]


def share_kernel(parts_ref, send_ref):
    rows, gain = merge(parts_ref[...].astype(F32))
    rows = rows.astype(BF16)
    tail = gain_rows(gain)
    for b in range(send_ref.shape[0]):
        send_ref[b, :GAIN_AT, :] = rows
        send_ref[b, GAIN_AT:, :] = tail


def adam_kernel(grad_ref, table_ref, first_ref, second_ref, new_table_ref, new_first_ref, new_second_ref, gain_ref):
    for b in range(grad_ref.shape[0]):
        tail = grad_ref[b, GAIN_AT:, :].astype(F32)
        for j in range(TILES):
            at = b * WIDE + j * L
            grad = grad_ref[b, j * ROWS : (j + 1) * ROWS, :].astype(F32)
            first = beta_first * first_ref[:, at : at + L] + (1.0 - beta_first) * grad
            second = beta_second * second_ref[:, at : at + L] + (1.0 - beta_second) * grad * grad
            update = learning_rate * (first / first_bias) / (jnp.sqrt(second / second_bias) + adam_epsilon)
            new_first_ref[:, at : at + L] = first
            new_second_ref[:, at : at + L] = second
            new_table_ref[:, at : at + L] = (table_ref[:, at : at + L].astype(F32) - update).astype(BF16)
            gain_ref[:, at : at + L] = tail[j : j + 1] + tail[TILES + j : TILES + j + 1]


def out_kernel(parts_ref, pick_ref, weights_ref, out_ref, score_ref, placed_grad_ref):
    step = pl.program_id(0)
    for b in range(MANY):
        for j in range(TILES):
            at = b * WIDE + j * L
            out_ref[:, at : at + L] = jnp.transpose(parts_ref[b, j * L : (j + 1) * L, :])
    part = sum(parts_ref[b, WIDE:, :].astype(F32) for b in range(MANY))

    @pl.when(step == 0)
    def _():
        placed_grad_ref[...] = part

    @pl.when(step > 0)
    def _():
        placed_grad_ref[...] += part

    @pl.when(step == pl.num_programs(0) - 1)
    def _():
        pick = pick_ref[...]
        weights = weights_ref[...]
        weight_grad = jnp.zeros((PICKS, TOK), F32)
        for m in range(SLOTS):
            weight_grad = jnp.where(pick == m, placed_grad_ref[m : m + 1, :], weight_grad)
        mean = jnp.sum(weights * weight_grad, axis=0, keepdims=True)
        score_ref[...] = weights * (weight_grad - mean)


def exchange(array, axes):
    return lax.all_to_all(array, axes, split_axis=0, concat_axis=0, tiled=True)


def swaps(array, axis, step):
    arrays = array if isinstance(array, (list, tuple)) else [array] * 4
    count = lax.axis_size(axis)
    return [arrays[0]] + [
        lax.ppermute(arrays[k], axis, [(i, i ^ (k * step)) for i in range(count)]) for k in range(1, 4)
    ]


def per_device(
    owners,
    pick_index,
    key_scores,
    output_cotangent,
    value_table,
    first_moment,
    second_moment,
    norm_gain,
):
    rows_x = lax.axis_size("x")
    steps = GROUP // STEP
    half = lax.axis_index("dl")
    block_index = half * RING + lax.axis_index("yc")

    yc = lax.axis_index("yc")
    place_here = jnp.stack([half, lax.axis_index("x"), yc // 2, yc % 2]).astype(jnp.int32)
    rows_y = RING // 2
    vmem = pl.BlockSpec(memory_space=pltpu.VMEM)
    smem = pl.BlockSpec(memory_space=pltpu.SMEM)

    def call(kernel, name, parts, outs):
        return pl.pallas_call(
            kernel,
            in_specs=[smem] + [vmem] * len(parts),
            out_specs=[vmem] * len(outs),
            out_shape=outs,
            compiler_params=PARAMS,
            name=name,
        )(place_here, *parts)

    whole = lambda *dims: pl.BlockSpec(dims, lambda i, *refs: (0,) * len(dims))

    batch_send, weights = pl.pallas_call(
        pack_kernel,
        grid=(GROUP // MANY,),
        in_specs=[
            whole(CANDS, TOK),
            whole(PICKS, TOK),
            whole(PICKS, TOK),
            pl.BlockSpec((TOK, MANY * WIDE), lambda i, *refs: (0, i)),
        ],
        out_specs=[pl.BlockSpec((MANY, WIDE + INFO, L), lambda i, *refs: (i, 0, 0)), whole(PICKS, TOK)],
        out_shape=(in_hbm(GROUP, WIDE + INFO, L, BF16), shape(PICKS, TOK, F32)),
        scratch_shapes=[pltpu.VMEM((INFO, TOK), BF16)],
        compiler_params=PARAMS,
        name="pack",
    )(owners.T, pick_index.T, key_scores.T, output_cotangent)
    batch_send, own_rows = lax.optimization_barrier((batch_send, value_table))
    batch = exchange(batch_send, ("dl", "yc"))

    same, other = pl.pallas_call(
        table_core_kernel,
        grid_spec=pltpu.PrefetchScalarGridSpec(
            num_scalar_prefetch=1,
            grid=(1,),
            in_specs=[pl.BlockSpec((ROWS, RING * WIDE), lambda i, place_ref: (0, place_ref[0]))],
            out_specs=[whole(rows_y, GAIN_AT, L)] * 2,
        ),
        out_shape=[shape(rows_y, GAIN_AT, L, BF16)] * 2,
        compiler_params=PARAMS,
        name="table_core",
    )(place_here, own_rows)
    got = lax.ppermute(other, "yc", [(i, i ^ 1) for i in range(RING)])
    pieces = call(table_y_kernel, "table_y", [same, got], [shape(2, GAIN_AT, L, BF16)] * rows_y)
    pieces = swaps(pieces, "yc", 2)
    (table,) = call(
        functools.partial(table_join_kernel, 2), "table_x", pieces, [shape(rows_y, 2, GAIN_AT, L, BF16)]
    )
    (table,) = call(
        functools.partial(table_join_kernel, 1),
        "table_all",
        swaps(table, "x", 1),
        [shape(rows_x, rows_y, 2, GAIN_AT, L, BF16)],
    )
    table = table.reshape(OWNERS, GAIN_AT, L)
    gain = lax.dynamic_slice(norm_gain, (block_index * WIDE,), (WIDE,)).reshape(WIDE, 1)

    batch_spec = pl.BlockSpec((STEP, WIDE + INFO, L), lambda i, *refs: (i, 0, 0))
    table_spec = whole(OWNERS, TILES * ROWS, L)
    wide_spec = pl.BlockSpec((WIDE, STEP * TOK), lambda i, *refs: (0, i))
    sums_spec = pl.BlockSpec((GROUP, 2, STEP * TOK), lambda i, *refs: (0, 0, i))
    tokens = GROUP * TOK

    memory, sums_send = pl.pallas_call(
        forward_kernel,
        grid=(steps,),
        in_specs=[batch_spec, table_spec, whole(WIDE, 1)],
        out_specs=[wide_spec, sums_spec],
        out_shape=(shape(WIDE, tokens, F32), shape(GROUP, 2, tokens, F32)),
        scratch_shapes=[pltpu.VMEM((WIDE, TABLE), BF16)],
        compiler_params=PARAMS,
        name="forward",
    )(batch, table, gain)
    sums = exchange(sums_send, ("dl", "yc"))

    out_turned, memory_grad, *pieces = pl.pallas_call(
        backward_kernel,
        grid_spec=pltpu.PrefetchScalarGridSpec(
            num_scalar_prefetch=1,
            grid=(steps,),
            in_specs=[batch_spec, whole(WIDE, 1), wide_spec, sums_spec],
            out_specs=[wide_spec, wide_spec] + [whole(RING * GAIN_AT + 8, L)] * rows_x,
            scratch_shapes=[pltpu.VMEM((TABLE, WIDE), F32), pltpu.VMEM((WIDE, L), F32)],
        ),
        out_shape=[shape(WIDE, tokens, BF16)] * 2 + [shape(RING * GAIN_AT + 8, L, BF16)] * rows_x,
        compiler_params=PARAMS,
        name="backward",
    )(place_here, batch, gain, memory, sums)

    back_send = pl.pallas_call(
        placed_grad_kernel,
        grid=(steps,),
        in_specs=[batch_spec, table_spec, wide_spec, wide_spec],
        out_specs=pl.BlockSpec((STEP, BACK, L), lambda i, *refs: (i, 0, 0)),
        out_shape=in_hbm(GROUP, BACK, L, BF16),
        compiler_params=PARAMS,
        name="placed_grad",
    )(batch, table, out_turned, memory_grad)

    back_send, pieces = lax.optimization_barrier((back_send, pieces))
    back = exchange(back_send, ("dl", "yc"))

    pieces = call(x_sum_kernel, "x_sum", swaps(pieces, "x", 1), [shape(2 * GAIN_AT + 8, L, BF16)] * rows_y)
    same, other = call(y_join_kernel, "y_join", swaps(pieces, "yc", 2), [shape(rows_y, GRAD, L, BF16)] * 2)
    got = lax.ppermute(other, "yc", [(i, i ^ 1) for i in range(RING)])
    (shares_send,) = call(plane_kernel, "plane_join", [same, got], [shape(RING, GRAD, L, BF16)])
    shares_send, back = lax.optimization_barrier((shares_send, back))
    shares = exchange(shares_send, "dh")
    total_send = pl.pallas_call(
        share_kernel,
        out_shape=shape(GROUP, GRAD, L, BF16),
        compiler_params=PARAMS,
        name="share_sum",
    )(shares)
    total = exchange(total_send, ("dl", "dh"))

    memory_out, score_turned = pl.pallas_call(
        out_kernel,
        grid=(GROUP // MANY,),
        in_specs=[pl.BlockSpec((MANY, BACK, L), lambda i, *refs: (i, 0, 0)), whole(PICKS, TOK), whole(PICKS, TOK)],
        out_specs=[pl.BlockSpec((TOK, MANY * WIDE), lambda i, *refs: (0, i)), whole(PICKS, TOK)],
        out_shape=(shape(TOK, D, BF16), shape(PICKS, TOK, F32)),
        scratch_shapes=[pltpu.VMEM((SLOTS, TOK), F32)],
        compiler_params=PARAMS,
        name="unpack",
    )(back, pick_index.T, weights)

    new_table, new_first, new_second, gain_gradient = pl.pallas_call(
        adam_kernel,
        out_shape=(
            shape(ROWS, D, BF16),
            shape(ROWS, D, F32),
            shape(ROWS, D, F32),
            shape(1, D, F32),
        ),
        compiler_params=PARAMS,
        name="adam",
    )(total, value_table, first_moment, second_moment)
    return (memory_out, score_turned.T, gain_gradient.reshape(D), new_table, new_first, new_second)


def solution(mesh):
    planes, mem_count = mesh.shape["dp"], mesh.shape["mem"]
    split_mesh = Mesh(
        mesh.devices.reshape(planes // PAIR, PAIR, mem_count // RING, RING), ("dh", "dl", "x", "yc")
    )
    tokens = P(("dh", "dl", "x", "yc"), None)
    rows = P(("x", "yc"), None)
    return jax.shard_map(
        per_device,
        mesh=split_mesh,
        in_specs=(tokens, tokens, tokens, tokens, rows, rows, rows, P()),
        out_specs=(tokens, tokens, P(), rows, rows, rows),
        check_vma=False,
    )
```

```python
import functools

import jax
import jax.numpy as jnp
from jax import lax
from jax.experimental import pallas as pl
from jax.experimental.pallas import tpu as pltpu
from jax.sharding import Mesh
from jax.sharding import PartitionSpec as P

beta_first = 0.9
beta_second = 0.95
learning_rate = 0.01
adam_epsilon = 1e-08
first_bias = 1.0 - (0.9**50) ** 2
second_bias = 1.0 - (0.95**50) ** 2
norm_epsilon = 1e-05

L = 128
PAIR = 2
RING = 8
GROUP = PAIR * RING
CANDS = 3
ROWS = 32
PICKS = 32
D = 4096
WIDE = D // GROUP
TILES = WIDE // L
TOK = 128
SLOTS = CANDS * ROWS
TABLE = 1024
OWNERS = TABLE // ROWS
INFO = SLOTS + 8
GAIN_AT = TILES * ROWS
GRAD = GAIN_AT + 8
BACK = WIDE + SLOTS
STEP = 4
MANY = 4
PLANE = ("xh", "xl", "yc")
TEAM = ("xl", "yc")
VMEM_LIMIT = 32 * 1024 * 1024
F32 = jnp.float32
BF16 = jnp.bfloat16
PARAMS = pltpu.CompilerParams(vmem_limit_bytes=VMEM_LIMIT)


def dot(a, b, dims):
    return lax.dot_general(a, b, (dims, ((), ())), preferred_element_type=F32)


def shape(*dims_and_type):
    return jax.ShapeDtypeStruct(dims_and_type[:-1], dims_and_type[-1])


def in_hbm(*dims_and_type):
    return pltpu.HBM(dims_and_type[:-1], dims_and_type[-1])


def table_kernel(table_ref, out_ref):
    for b in range(GROUP):
        for j in range(TILES):
            at = b * WIDE + j * L
            tile = table_ref[:, at : at + L]
            for x in range(out_ref.shape[0]):
                out_ref[x, b, j * ROWS : (j + 1) * ROWS, :] = tile


def pack_kernel(owners_ref, pick_ref, scores_ref, cotangent_ref, send_ref, weights_ref, info_ref):
    @pl.when(pl.program_id(0) == 0)
    def _():
        scores = scores_ref[...]
        shifted = jnp.exp(scores - jnp.max(scores, axis=0, keepdims=True))
        weights = shifted / jnp.sum(shifted, axis=0, keepdims=True)
        weights_ref[...] = weights
        pick = pick_ref[...]
        entry = lax.broadcasted_iota(jnp.int32, (SLOTS, TOK), 0)
        placed = jnp.zeros((SLOTS, TOK), F32)
        for k in range(PICKS):
            placed = jnp.where(pick[k : k + 1] == entry, weights[k : k + 1], placed)
        owners = owners_ref[...].astype(F32)
        line = lax.broadcasted_iota(jnp.int32, (8, TOK), 0)
        named = jnp.zeros((8, TOK), F32)
        for c in range(CANDS):
            named = jnp.where(line == c, owners[c : c + 1], named)
        info_ref[...] = jnp.concatenate([placed, named], axis=0).astype(BF16)

    for b in range(MANY):
        for j in range(TILES):
            at = b * WIDE + j * L
            send_ref[b, j * L : (j + 1) * L, :] = jnp.transpose(cotangent_ref[:, at : at + L])
        send_ref[b, WIDE:, :] = info_ref[...]


def load_info(batch_ref):
    info = jnp.concatenate([batch_ref[i, WIDE:, :] for i in range(STEP)], axis=1).astype(F32)
    placed = [info[c * ROWS : (c + 1) * ROWS] for c in range(CANDS)]
    named = [
        jnp.broadcast_to(info[SLOTS + c : SLOTS + c + 1], (ROWS, STEP * TOK)) for c in range(CANDS)
    ]
    return placed, named


def place(placed, named):
    blocks = []
    for o in range(OWNERS):
        block = jnp.zeros((ROWS, STEP * TOK), F32)
        for c in range(CANDS):
            block = jnp.where(named[c] == float(o), placed[c], block)
        blocks.append(block.astype(BF16))
    return jnp.concatenate(blocks, axis=0)


def load_table(table_ref):
    return jnp.concatenate(
        [table_ref[:, j * ROWS : (j + 1) * ROWS, :].reshape(TABLE, L) for j in range(TILES)], axis=1
    )


def load_cotangent(batch_ref):
    return jnp.concatenate([batch_ref[i, :WIDE, :] for i in range(STEP)], axis=1).astype(F32)


def forward_kernel(batch_ref, table_ref, gain_ref, memory_ref, sums_ref, turned_ref):
    @pl.when(pl.program_id(0) == 0)
    def _():
        turned_ref[...] = jnp.transpose(load_table(table_ref))

    memory = dot(turned_ref[...], place(*load_info(batch_ref)), ((1,), (0,)))
    memory_ref[...] = memory
    scaled = load_cotangent(batch_ref) * gain_ref[...]
    square = jnp.sum(memory * memory, axis=0, keepdims=True)
    cross = jnp.sum(scaled * memory, axis=0, keepdims=True)
    both = jnp.concatenate([square, cross], axis=0)
    for g in range(sums_ref.shape[0]):
        sums_ref[g] = both


def split(value):
    high = value.astype(BF16).astype(F32)
    return high, value - high


def gain_rows(rows):
    high, low = split(rows)
    return jnp.concatenate([high, low, jnp.zeros((8 - 2 * TILES, L), F32)], axis=0).astype(BF16)


def backward_kernel(batch_ref, gain_ref, memory_ref, sums_ref, out_ref, grad_ref, send_ref, total_ref, gain_sum_ref):
    step = pl.program_id(0)
    sums = jnp.sum(sums_ref[...], axis=0)
    inverse = lax.rsqrt(sums[0:1] / D + norm_epsilon)
    factor = inverse * inverse * inverse * (sums[1:2] / D)
    memory = memory_ref[...]
    cotangent = load_cotangent(batch_ref)
    gain = gain_ref[...]
    normed = memory * inverse
    out_ref[...] = (normed * gain).astype(BF16)
    grad = (inverse * (cotangent * gain) - memory * factor).astype(BF16)
    grad_ref[...] = grad
    gain_part = cotangent * normed
    folded = sum(gain_part[:, i * L : (i + 1) * L] for i in range(STEP))
    table_part = dot(place(*load_info(batch_ref)), grad, ((1,), (1,)))

    @pl.when(step == 0)
    def _():
        total_ref[...] = table_part
        gain_sum_ref[...] = folded

    @pl.when(step > 0)
    def _():
        total_ref[...] += table_part
        gain_sum_ref[...] += folded

    @pl.when(step == pl.num_programs(0) - 1)
    def _():
        for j in range(TILES):
            send_ref[:, j * ROWS : (j + 1) * ROWS, :] = (
                total_ref[:, j * L : (j + 1) * L].astype(BF16).reshape(OWNERS, ROWS, L)
            )
        turned = jnp.transpose(gain_sum_ref[...])
        rows = [jnp.sum(turned[:, j * L : (j + 1) * L], axis=0, keepdims=True) for j in range(TILES)]
        tail = gain_rows(jnp.concatenate(rows, axis=0))
        for o in range(OWNERS):
            send_ref[o, GAIN_AT:, :] = tail


def placed_grad_kernel(batch_ref, table_ref, out_ref, grad_ref, send_ref):
    _, named = load_info(batch_ref)
    full = dot(load_table(table_ref), grad_ref[...], ((1,), (0,)))
    found = [jnp.zeros((ROWS, STEP * TOK), F32) for _ in range(CANDS)]
    for o in range(OWNERS):
        block = full[o * ROWS : (o + 1) * ROWS]
        for c in range(CANDS):
            found[c] = jnp.where(named[c] == float(o), block, found[c])
    for i in range(STEP):
        send_ref[i, :WIDE, :] = out_ref[:, i * TOK : (i + 1) * TOK]
        for c in range(CANDS):
            send_ref[i, WIDE + c * ROWS : WIDE + (c + 1) * ROWS, :] = found[c][
                :, i * TOK : (i + 1) * TOK
            ].astype(BF16)


def merge(parts):
    total = jnp.sum(parts, axis=0)
    gain = total[GAIN_AT : GAIN_AT + TILES] + total[GAIN_AT + TILES : GAIN_AT + 2 * TILES]
    return total[:GAIN_AT], gain


def plane_kernel(parts_ref, send_ref):
    for b in range(parts_ref.shape[1]):
        rows, gain = merge(parts_ref[:, b].astype(F32))
        send_ref[b, :GAIN_AT, :] = rows.astype(BF16)
        send_ref[b, GAIN_AT:, :] = gain_rows(gain)


def share_kernel(parts_ref, send_ref):
    rows, gain = merge(parts_ref[...].astype(F32))
    send_ref[:GAIN_AT, :] = rows.astype(BF16)
    send_ref[GAIN_AT:, :] = gain_rows(gain)


def adam_kernel(grad_ref, table_ref, first_ref, second_ref, new_table_ref, new_first_ref, new_second_ref, gain_ref):
    for b in range(grad_ref.shape[0]):
        tail = grad_ref[b, GAIN_AT:, :].astype(F32)
        for j in range(TILES):
            at = b * WIDE + j * L
            grad = grad_ref[b, j * ROWS : (j + 1) * ROWS, :].astype(F32)
            first = beta_first * first_ref[:, at : at + L] + (1.0 - beta_first) * grad
            second = beta_second * second_ref[:, at : at + L] + (1.0 - beta_second) * grad * grad
            update = learning_rate * (first / first_bias) / (jnp.sqrt(second / second_bias) + adam_epsilon)
            new_first_ref[:, at : at + L] = first
            new_second_ref[:, at : at + L] = second
            new_table_ref[:, at : at + L] = (table_ref[:, at : at + L].astype(F32) - update).astype(BF16)
            gain_ref[:, at : at + L] = tail[j : j + 1] + tail[TILES + j : TILES + j + 1]


def out_kernel(parts_ref, pick_ref, weights_ref, out_ref, score_ref, placed_grad_ref):
    step = pl.program_id(0)
    for b in range(MANY):
        for j in range(TILES):
            at = b * WIDE + j * L
            out_ref[:, at : at + L] = jnp.transpose(parts_ref[b, j * L : (j + 1) * L, :])
    part = sum(parts_ref[b, WIDE:, :].astype(F32) for b in range(MANY))

    @pl.when(step == 0)
    def _():
        placed_grad_ref[...] = part

    @pl.when(step > 0)
    def _():
        placed_grad_ref[...] += part

    @pl.when(step == pl.num_programs(0) - 1)
    def _():
        pick = pick_ref[...]
        weights = weights_ref[...]
        weight_grad = jnp.zeros((PICKS, TOK), F32)
        for m in range(SLOTS):
            weight_grad = jnp.where(pick == m, placed_grad_ref[m : m + 1, :], weight_grad)
        mean = jnp.sum(weights * weight_grad, axis=0, keepdims=True)
        score_ref[...] = weights * (weight_grad - mean)


def exchange(array, axes):
    return lax.all_to_all(array, axes, split_axis=0, concat_axis=0, tiled=True)


def per_device(
    owners,
    pick_index,
    key_scores,
    output_cotangent,
    value_table,
    first_moment,
    second_moment,
    norm_gain,
):
    groups = lax.axis_size("xh")
    steps = GROUP // STEP
    block_index = lax.axis_index(TEAM)

    whole = lambda *dims: pl.BlockSpec(dims, lambda i: (0,) * len(dims))

    table_send = pl.pallas_call(
        table_kernel,
        out_shape=in_hbm(groups, GROUP, TILES * ROWS, L, BF16),
        compiler_params=PARAMS,
        name="table_send",
    )(value_table)
    table = exchange(table_send.reshape(OWNERS, TILES * ROWS, L), PLANE)

    batch_send, weights = pl.pallas_call(
        pack_kernel,
        grid=(GROUP // MANY,),
        in_specs=[
            whole(CANDS, TOK),
            whole(PICKS, TOK),
            whole(PICKS, TOK),
            pl.BlockSpec((TOK, MANY * WIDE), lambda i: (0, i)),
        ],
        out_specs=[pl.BlockSpec((MANY, WIDE + INFO, L), lambda i: (i, 0, 0)), whole(PICKS, TOK)],
        out_shape=(in_hbm(GROUP, WIDE + INFO, L, BF16), shape(PICKS, TOK, F32)),
        scratch_shapes=[pltpu.VMEM((INFO, TOK), BF16)],
        compiler_params=PARAMS,
        name="pack",
    )(owners.T, pick_index.T, key_scores.T, output_cotangent)
    batch = exchange(batch_send, TEAM)
    gain = lax.dynamic_slice(norm_gain, (block_index * WIDE,), (WIDE,)).reshape(WIDE, 1)

    batch_spec = pl.BlockSpec((STEP, WIDE + INFO, L), lambda i: (i, 0, 0))
    table_spec = whole(OWNERS, TILES * ROWS, L)
    wide_spec = pl.BlockSpec((WIDE, STEP * TOK), lambda i: (0, i))
    sums_spec = pl.BlockSpec((GROUP, 2, STEP * TOK), lambda i: (0, 0, i))
    tokens = GROUP * TOK

    memory, sums_send = pl.pallas_call(
        forward_kernel,
        grid=(steps,),
        in_specs=[batch_spec, table_spec, whole(WIDE, 1)],
        out_specs=[wide_spec, sums_spec],
        out_shape=(shape(WIDE, tokens, F32), shape(GROUP, 2, tokens, F32)),
        scratch_shapes=[pltpu.VMEM((WIDE, TABLE), BF16)],
        compiler_params=PARAMS,
        name="forward",
    )(batch, table, gain)
    sums = exchange(sums_send, TEAM)

    out_turned, memory_grad, grad_send = pl.pallas_call(
        backward_kernel,
        grid=(steps,),
        in_specs=[batch_spec, whole(WIDE, 1), wide_spec, sums_spec],
        out_specs=[wide_spec, wide_spec, whole(OWNERS, GRAD, L)],
        out_shape=(
            in_hbm(WIDE, tokens, BF16),
            in_hbm(WIDE, tokens, BF16),
            in_hbm(OWNERS, GRAD, L, BF16),
        ),
        scratch_shapes=[pltpu.VMEM((TABLE, WIDE), F32), pltpu.VMEM((WIDE, L), F32)],
        compiler_params=PARAMS,
        name="backward",
    )(batch, gain, memory, sums)
    plane_parts = exchange(grad_send, PLANE)

    back_send = pl.pallas_call(
        placed_grad_kernel,
        grid=(steps,),
        in_specs=[batch_spec, table_spec, wide_spec, wide_spec],
        out_specs=pl.BlockSpec((STEP, BACK, L), lambda i: (i, 0, 0)),
        out_shape=in_hbm(GROUP, BACK, L, BF16),
        compiler_params=PARAMS,
        name="placed_grad",
    )(batch, table, out_turned, memory_grad)

    plane_parts, back_send = lax.optimization_barrier((plane_parts, back_send))
    shares_send = pl.pallas_call(
        plane_kernel,
        out_shape=shape(GROUP, GRAD, L, BF16),
        compiler_params=PARAMS,
        name="plane_sum",
    )(plane_parts.reshape(groups, GROUP, GRAD, L))
    shares = exchange(shares_send, "dp")
    total = pl.pallas_call(
        share_kernel,
        out_shape=shape(GRAD, L, BF16),
        compiler_params=PARAMS,
        name="share_sum",
    )(shares)
    total, back_send = lax.optimization_barrier((total, back_send))
    totals = lax.all_gather(total, "dp", axis=0, tiled=False)

    back = exchange(back_send, TEAM)
    memory_out, score_turned = pl.pallas_call(
        out_kernel,
        grid=(GROUP // MANY,),
        in_specs=[pl.BlockSpec((MANY, BACK, L), lambda i: (i, 0, 0)), whole(PICKS, TOK), whole(PICKS, TOK)],
        out_specs=[pl.BlockSpec((TOK, MANY * WIDE), lambda i: (0, i)), whole(PICKS, TOK)],
        out_shape=(shape(TOK, D, BF16), shape(PICKS, TOK, F32)),
        scratch_shapes=[pltpu.VMEM((SLOTS, TOK), F32)],
        compiler_params=PARAMS,
        name="unpack",
    )(back, pick_index.T, weights)

    new_table, new_first, new_second, gain_gradient = pl.pallas_call(
        adam_kernel,
        out_shape=(
            shape(ROWS, D, BF16),
            shape(ROWS, D, F32),
            shape(ROWS, D, F32),
            shape(1, D, F32),
        ),
        compiler_params=PARAMS,
        name="adam",
    )(totals, value_table, first_moment, second_moment)
    return (memory_out, score_turned.T, gain_gradient.reshape(D), new_table, new_first, new_second)


def solution(mesh):
    planes, mem_count = mesh.shape["dp"], mesh.shape["mem"]
    split_mesh = Mesh(mesh.devices.reshape(planes, mem_count // GROUP, PAIR, RING), ("dp",) + PLANE)
    tokens = P(("dp",) + PLANE, None)
    rows = P(PLANE, None)
    return jax.shard_map(
        per_device,
        mesh=split_mesh,
        in_specs=(tokens, tokens, tokens, tokens, rows, rows, rows, P()),
        out_specs=(tokens, tokens, P(), rows, rows, rows),
        check_vma=False,
    )
```

```python
import functools

import jax
import jax.numpy as jnp
from jax import lax
from jax.experimental import pallas as pl
from jax.experimental.pallas import tpu as pltpu
from jax.sharding import Mesh
from jax.sharding import PartitionSpec as P

beta_first = 0.9
beta_second = 0.95
learning_rate = 0.01
adam_epsilon = 1e-08
first_bias = 1.0 - (0.9**50) ** 2
second_bias = 1.0 - (0.95**50) ** 2
norm_epsilon = 1e-05

L = 128
PAIR = 2
RING = 8
GROUP = PAIR * RING
CANDS = 3
ROWS = 32
PICKS = 32
D = 4096
WIDE = D // GROUP
TILES = WIDE // L
TOK = 128
SLOTS = CANDS * ROWS
TABLE = 1024
OWNERS = TABLE // ROWS
INFO = SLOTS + 8
GAIN_AT = TILES * ROWS
GRAD = GAIN_AT + 8
BACK = WIDE + SLOTS
STEP = 4
MANY = 4
PLANE = ("xh", "xl", "yc")
TEAM = ("xl", "yc")
VMEM_LIMIT = 32 * 1024 * 1024
F32 = jnp.float32
BF16 = jnp.bfloat16
PARAMS = pltpu.CompilerParams(vmem_limit_bytes=VMEM_LIMIT)


def dot(a, b, dims):
    return lax.dot_general(a, b, (dims, ((), ())), preferred_element_type=F32)


def shape(*dims_and_type):
    return jax.ShapeDtypeStruct(dims_and_type[:-1], dims_and_type[-1])


def in_hbm(*dims_and_type):
    return pltpu.HBM(dims_and_type[:-1], dims_and_type[-1])


def table_kernel(table_ref, out_ref):
    for b in range(GROUP):
        for j in range(TILES):
            at = b * WIDE + j * L
            out_ref[b, j * ROWS : (j + 1) * ROWS, :] = table_ref[:, at : at + L]


def join_kernel(place_ref, own_ref, other_ref, out_ref):
    out_ref[place_ref[0]] = own_ref[...]
    out_ref[1 - place_ref[0]] = other_ref[...]


def pack_kernel(owners_ref, pick_ref, scores_ref, cotangent_ref, send_ref, weights_ref, info_ref):
    @pl.when(pl.program_id(0) == 0)
    def _():
        scores = scores_ref[...]
        shifted = jnp.exp(scores - jnp.max(scores, axis=0, keepdims=True))
        weights = shifted / jnp.sum(shifted, axis=0, keepdims=True)
        weights_ref[...] = weights
        pick = pick_ref[...]
        entry = lax.broadcasted_iota(jnp.int32, (SLOTS, TOK), 0)
        placed = jnp.zeros((SLOTS, TOK), F32)
        for k in range(PICKS):
            placed = jnp.where(pick[k : k + 1] == entry, weights[k : k + 1], placed)
        owners = owners_ref[...].astype(F32)
        line = lax.broadcasted_iota(jnp.int32, (8, TOK), 0)
        named = jnp.zeros((8, TOK), F32)
        for c in range(CANDS):
            named = jnp.where(line == c, owners[c : c + 1], named)
        info_ref[...] = jnp.concatenate([placed, named], axis=0).astype(BF16)

    for b in range(MANY):
        for j in range(TILES):
            at = b * WIDE + j * L
            send_ref[b, j * L : (j + 1) * L, :] = jnp.transpose(cotangent_ref[:, at : at + L])
        send_ref[b, WIDE:, :] = info_ref[...]


def load_info(batch_ref):
    info = jnp.concatenate([batch_ref[i, WIDE:, :] for i in range(STEP)], axis=1).astype(F32)
    placed = [info[c * ROWS : (c + 1) * ROWS] for c in range(CANDS)]
    named = [
        jnp.broadcast_to(info[SLOTS + c : SLOTS + c + 1], (ROWS, STEP * TOK)) for c in range(CANDS)
    ]
    return placed, named


def place(placed, named):
    blocks = []
    for o in range(OWNERS):
        block = jnp.zeros((ROWS, STEP * TOK), F32)
        for c in range(CANDS):
            block = jnp.where(named[c] == float(o), placed[c], block)
        blocks.append(block.astype(BF16))
    return jnp.concatenate(blocks, axis=0)


def load_table(table_ref):
    return jnp.concatenate(
        [table_ref[:, j * ROWS : (j + 1) * ROWS, :].reshape(TABLE, L) for j in range(TILES)], axis=1
    )


def load_cotangent(batch_ref):
    return jnp.concatenate([batch_ref[i, :WIDE, :] for i in range(STEP)], axis=1).astype(F32)


def forward_kernel(batch_ref, table_ref, gain_ref, memory_ref, sums_ref, turned_ref):
    @pl.when(pl.program_id(0) == 0)
    def _():
        turned_ref[...] = jnp.transpose(load_table(table_ref))

    memory = dot(turned_ref[...], place(*load_info(batch_ref)), ((1,), (0,)))
    memory_ref[...] = memory
    scaled = load_cotangent(batch_ref) * gain_ref[...]
    square = jnp.sum(memory * memory, axis=0, keepdims=True)
    cross = jnp.sum(scaled * memory, axis=0, keepdims=True)
    both = jnp.concatenate([square, cross], axis=0)
    for g in range(sums_ref.shape[0]):
        sums_ref[g] = both


def split(value):
    high = value.astype(BF16).astype(F32)
    return high, value - high


def gain_rows(rows):
    high, low = split(rows)
    return jnp.concatenate([high, low, jnp.zeros((8 - 2 * TILES, L), F32)], axis=0).astype(BF16)


def backward_kernel(batch_ref, gain_ref, memory_ref, sums_ref, out_ref, grad_ref, send_ref, total_ref, gain_sum_ref):
    step = pl.program_id(0)
    sums = jnp.sum(sums_ref[...], axis=0)
    inverse = lax.rsqrt(sums[0:1] / D + norm_epsilon)
    factor = inverse * inverse * inverse * (sums[1:2] / D)
    memory = memory_ref[...]
    cotangent = load_cotangent(batch_ref)
    gain = gain_ref[...]
    normed = memory * inverse
    out_ref[...] = (normed * gain).astype(BF16)
    grad = (inverse * (cotangent * gain) - memory * factor).astype(BF16)
    grad_ref[...] = grad
    gain_part = cotangent * normed
    folded = sum(gain_part[:, i * L : (i + 1) * L] for i in range(STEP))
    table_part = dot(place(*load_info(batch_ref)), grad, ((1,), (1,)))

    @pl.when(step == 0)
    def _():
        total_ref[...] = table_part
        gain_sum_ref[...] = folded

    @pl.when(step > 0)
    def _():
        total_ref[...] += table_part
        gain_sum_ref[...] += folded

    @pl.when(step == pl.num_programs(0) - 1)
    def _():
        for j in range(TILES):
            send_ref[:, j * ROWS : (j + 1) * ROWS, :] = (
                total_ref[:, j * L : (j + 1) * L].astype(BF16).reshape(OWNERS, ROWS, L)
            )
        turned = jnp.transpose(gain_sum_ref[...])
        rows = [jnp.sum(turned[:, j * L : (j + 1) * L], axis=0, keepdims=True) for j in range(TILES)]
        tail = gain_rows(jnp.concatenate(rows, axis=0))
        for o in range(OWNERS):
            send_ref[o, GAIN_AT:, :] = tail


def placed_grad_kernel(batch_ref, table_ref, out_ref, grad_ref, send_ref):
    _, named = load_info(batch_ref)
    full = dot(load_table(table_ref), grad_ref[...], ((1,), (0,)))
    found = [jnp.zeros((ROWS, STEP * TOK), F32) for _ in range(CANDS)]
    for o in range(OWNERS):
        block = full[o * ROWS : (o + 1) * ROWS]
        for c in range(CANDS):
            found[c] = jnp.where(named[c] == float(o), block, found[c])
    for i in range(STEP):
        send_ref[i, :WIDE, :] = out_ref[:, i * TOK : (i + 1) * TOK]
        for c in range(CANDS):
            send_ref[i, WIDE + c * ROWS : WIDE + (c + 1) * ROWS, :] = found[c][
                :, i * TOK : (i + 1) * TOK
            ].astype(BF16)


def merge(parts):
    total = jnp.sum(parts, axis=0)
    gain = total[GAIN_AT : GAIN_AT + TILES] + total[GAIN_AT + TILES : GAIN_AT + 2 * TILES]
    return total[:GAIN_AT], gain


def plane_kernel(parts_ref, send_ref):
    for b in range(parts_ref.shape[1]):
        rows, gain = merge(parts_ref[:, b].astype(F32))
        send_ref[b, :GAIN_AT, :] = rows.astype(BF16)
        send_ref[b, GAIN_AT:, :] = gain_rows(gain)


def share_kernel(parts_ref, send_ref):
    rows, gain = merge(parts_ref[...].astype(F32))
    send_ref[:GAIN_AT, :] = rows.astype(BF16)
    send_ref[GAIN_AT:, :] = gain_rows(gain)


def adam_kernel(grad_ref, table_ref, first_ref, second_ref, new_table_ref, new_first_ref, new_second_ref, gain_ref):
    for b in range(grad_ref.shape[0]):
        tail = grad_ref[b, GAIN_AT:, :].astype(F32)
        for j in range(TILES):
            at = b * WIDE + j * L
            grad = grad_ref[b, j * ROWS : (j + 1) * ROWS, :].astype(F32)
            first = beta_first * first_ref[:, at : at + L] + (1.0 - beta_first) * grad
            second = beta_second * second_ref[:, at : at + L] + (1.0 - beta_second) * grad * grad
            update = learning_rate * (first / first_bias) / (jnp.sqrt(second / second_bias) + adam_epsilon)
            new_first_ref[:, at : at + L] = first
            new_second_ref[:, at : at + L] = second
            new_table_ref[:, at : at + L] = (table_ref[:, at : at + L].astype(F32) - update).astype(BF16)
            gain_ref[:, at : at + L] = tail[j : j + 1] + tail[TILES + j : TILES + j + 1]


def out_kernel(parts_ref, pick_ref, weights_ref, out_ref, score_ref, placed_grad_ref):
    step = pl.program_id(0)
    for b in range(MANY):
        for j in range(TILES):
            at = b * WIDE + j * L
            out_ref[:, at : at + L] = jnp.transpose(parts_ref[b, j * L : (j + 1) * L, :])
    part = sum(parts_ref[b, WIDE:, :].astype(F32) for b in range(MANY))

    @pl.when(step == 0)
    def _():
        placed_grad_ref[...] = part

    @pl.when(step > 0)
    def _():
        placed_grad_ref[...] += part

    @pl.when(step == pl.num_programs(0) - 1)
    def _():
        pick = pick_ref[...]
        weights = weights_ref[...]
        weight_grad = jnp.zeros((PICKS, TOK), F32)
        for m in range(SLOTS):
            weight_grad = jnp.where(pick == m, placed_grad_ref[m : m + 1, :], weight_grad)
        mean = jnp.sum(weights * weight_grad, axis=0, keepdims=True)
        score_ref[...] = weights * (weight_grad - mean)


def last_kernel(
    parts_ref, pick_ref, weights_ref, grad_ref, table_ref, first_ref, second_ref,
    out_ref, score_ref, new_table_ref, new_first_ref, new_second_ref, gain_ref, placed_grad_ref,
):
    adam_kernel(grad_ref, table_ref, first_ref, second_ref, new_table_ref, new_first_ref, new_second_ref, gain_ref)
    out_kernel(parts_ref, pick_ref, weights_ref, out_ref, score_ref, placed_grad_ref)


def exchange(array, axes):
    return lax.all_to_all(array, axes, split_axis=0, concat_axis=0, tiled=True)


def per_device(
    owners,
    pick_index,
    key_scores,
    output_cotangent,
    value_table,
    first_moment,
    second_moment,
    norm_gain,
):
    groups = lax.axis_size("xh")
    steps = GROUP // STEP
    block_index = lax.axis_index(TEAM)

    whole = lambda *dims: pl.BlockSpec(dims, lambda i: (0,) * len(dims))

    table_send = pl.pallas_call(
        table_kernel,
        out_shape=in_hbm(GROUP, TILES * ROWS, L, BF16),
        compiler_params=PARAMS,
        name="table_send",
    )(value_table)
    own_half = exchange(table_send, TEAM)

    batch_send, weights = pl.pallas_call(
        pack_kernel,
        grid=(GROUP // MANY,),
        in_specs=[
            whole(CANDS, TOK),
            whole(PICKS, TOK),
            whole(PICKS, TOK),
            pl.BlockSpec((TOK, MANY * WIDE), lambda i: (0, i)),
        ],
        out_specs=[pl.BlockSpec((MANY, WIDE + INFO, L), lambda i: (i, 0, 0)), whole(PICKS, TOK)],
        out_shape=(in_hbm(GROUP, WIDE + INFO, L, BF16), shape(PICKS, TOK, F32)),
        scratch_shapes=[pltpu.VMEM((INFO, TOK), BF16)],
        compiler_params=PARAMS,
        name="pack",
    )(owners.T, pick_index.T, key_scores.T, output_cotangent)
    own_half, batch_send = lax.optimization_barrier((own_half, batch_send))
    batch = exchange(batch_send, TEAM)
    other_half = lax.ppermute(own_half, "xh", [(i, (i + 1) % groups) for i in range(groups)])
    vmem = pl.BlockSpec(memory_space=pltpu.VMEM)
    table = pl.pallas_call(
        join_kernel,
        in_specs=[pl.BlockSpec(memory_space=pltpu.SMEM), vmem, vmem],
        out_specs=vmem,
        out_shape=shape(groups, GROUP, TILES * ROWS, L, BF16),
        compiler_params=PARAMS,
        name="table_join",
    )(lax.axis_index("xh").reshape(1).astype(jnp.int32), own_half, other_half)
    table = table.reshape(OWNERS, TILES * ROWS, L)
    gain = lax.dynamic_slice(norm_gain, (block_index * WIDE,), (WIDE,)).reshape(WIDE, 1)

    batch_spec = pl.BlockSpec((STEP, WIDE + INFO, L), lambda i: (i, 0, 0))
    table_spec = whole(OWNERS, TILES * ROWS, L)
    wide_spec = pl.BlockSpec((WIDE, STEP * TOK), lambda i: (0, i))
    sums_spec = pl.BlockSpec((GROUP, 2, STEP * TOK), lambda i: (0, 0, i))
    tokens = GROUP * TOK

    memory, sums_send = pl.pallas_call(
        forward_kernel,
        grid=(steps,),
        in_specs=[batch_spec, table_spec, whole(WIDE, 1)],
        out_specs=[wide_spec, sums_spec],
        out_shape=(shape(WIDE, tokens, F32), shape(GROUP, 2, tokens, F32)),
        scratch_shapes=[pltpu.VMEM((WIDE, TABLE), BF16)],
        compiler_params=PARAMS,
        name="forward",
    )(batch, table, gain)
    sums = exchange(sums_send, TEAM)

    out_turned, memory_grad, grad_send = pl.pallas_call(
        backward_kernel,
        grid=(steps,),
        in_specs=[batch_spec, whole(WIDE, 1), wide_spec, sums_spec],
        out_specs=[wide_spec, wide_spec, whole(OWNERS, GRAD, L)],
        out_shape=(
            in_hbm(WIDE, tokens, BF16),
            in_hbm(WIDE, tokens, BF16),
            in_hbm(OWNERS, GRAD, L, BF16),
        ),
        scratch_shapes=[pltpu.VMEM((TABLE, WIDE), F32), pltpu.VMEM((WIDE, L), F32)],
        compiler_params=PARAMS,
        name="backward",
    )(batch, gain, memory, sums)
    plane_parts = exchange(grad_send, PLANE)

    back_send = pl.pallas_call(
        placed_grad_kernel,
        grid=(steps,),
        in_specs=[batch_spec, table_spec, wide_spec, wide_spec],
        out_specs=pl.BlockSpec((STEP, BACK, L), lambda i: (i, 0, 0)),
        out_shape=in_hbm(GROUP, BACK, L, BF16),
        compiler_params=PARAMS,
        name="placed_grad",
    )(batch, table, out_turned, memory_grad)

    plane_parts, back_send = lax.optimization_barrier((plane_parts, back_send))
    shares_send = pl.pallas_call(
        plane_kernel,
        out_shape=shape(GROUP, GRAD, L, BF16),
        compiler_params=PARAMS,
        name="plane_sum",
    )(plane_parts.reshape(groups, GROUP, GRAD, L))
    shares = exchange(shares_send, "dp")
    total = pl.pallas_call(
        share_kernel,
        out_shape=shape(GRAD, L, BF16),
        compiler_params=PARAMS,
        name="share_sum",
    )(shares)
    total, back_send = lax.optimization_barrier((total, back_send))
    totals = lax.all_gather(total, "dp", axis=0, tiled=False)

    back = exchange(back_send, TEAM)
    rows_spec = pl.BlockSpec((ROWS, MANY * WIDE), lambda i: (0, i))
    memory_out, score_turned, new_table, new_first, new_second, gain_gradient = pl.pallas_call(
        last_kernel,
        grid=(GROUP // MANY,),
        in_specs=[
            pl.BlockSpec((MANY, BACK, L), lambda i: (i, 0, 0)),
            whole(PICKS, TOK),
            whole(PICKS, TOK),
            pl.BlockSpec((MANY, GRAD, L), lambda i: (i, 0, 0)),
            rows_spec,
            rows_spec,
            rows_spec,
        ],
        out_specs=[
            pl.BlockSpec((TOK, MANY * WIDE), lambda i: (0, i)),
            whole(PICKS, TOK),
            rows_spec,
            rows_spec,
            rows_spec,
            pl.BlockSpec((1, MANY * WIDE), lambda i: (0, i)),
        ],
        out_shape=(
            shape(TOK, D, BF16),
            shape(PICKS, TOK, F32),
            shape(ROWS, D, BF16),
            shape(ROWS, D, F32),
            shape(ROWS, D, F32),
            shape(1, D, F32),
        ),
        scratch_shapes=[pltpu.VMEM((SLOTS, TOK), F32)],
        compiler_params=PARAMS,
        name="last",
    )(back, pick_index.T, weights, totals, value_table, first_moment, second_moment)
    return (memory_out, score_turned.T, gain_gradient.reshape(D), new_table, new_first, new_second)


def solution(mesh):
    planes, mem_count = mesh.shape["dp"], mesh.shape["mem"]
    split_mesh = Mesh(mesh.devices.reshape(planes, mem_count // GROUP, PAIR, RING), ("dp",) + PLANE)
    tokens = P(("dp",) + PLANE, None)
    rows = P(PLANE, None)
    return jax.shard_map(
        per_device,
        mesh=split_mesh,
        in_specs=(tokens, tokens, tokens, tokens, rows, rows, rows, P()),
        out_specs=(tokens, tokens, P(), rows, rows, rows),
        check_vma=False,
    )
```

```python
import functools

import jax
import jax.numpy as jnp
from jax import lax
from jax.experimental import pallas as pl
from jax.experimental.pallas import tpu as pltpu
from jax.sharding import Mesh
from jax.sharding import PartitionSpec as P

beta_first = 0.9
beta_second = 0.95
learning_rate = 0.01
adam_epsilon = 1e-08
first_bias = 1.0 - (0.9**50) ** 2
second_bias = 1.0 - (0.95**50) ** 2
norm_epsilon = 1e-05

L = 128
PAIR = 2
RING = 8
GROUP = PAIR * RING
CANDS = 3
ROWS = 32
PICKS = 32
D = 4096
WIDE = D // GROUP
TILES = WIDE // L
TOK = 128
SLOTS = CANDS * ROWS
TABLE = 1024
OWNERS = TABLE // ROWS
INFO = SLOTS + 8
GAIN_AT = TILES * ROWS
GRAD = GAIN_AT + 8
BACK = WIDE + SLOTS
STEP = 4
MANY = 4
PLANE = ("xh", "xl", "yc")
TEAM = ("xl", "yc")
VMEM_LIMIT = 32 * 1024 * 1024
F32 = jnp.float32
BF16 = jnp.bfloat16
PARAMS = pltpu.CompilerParams(vmem_limit_bytes=VMEM_LIMIT)


def dot(a, b, dims):
    return lax.dot_general(a, b, (dims, ((), ())), preferred_element_type=F32)


def shape(*dims_and_type):
    return jax.ShapeDtypeStruct(dims_and_type[:-1], dims_and_type[-1])


def in_hbm(*dims_and_type):
    return pltpu.HBM(dims_and_type[:-1], dims_and_type[-1])


def table_kernel(table_ref, out_ref):
    for b in range(GROUP):
        for j in range(TILES):
            at = b * WIDE + j * L
            tile = table_ref[:, at : at + L]
            for x in range(out_ref.shape[0]):
                out_ref[x, b, j * ROWS : (j + 1) * ROWS, :] = tile


def pack_kernel(owners_ref, pick_ref, scores_ref, cotangent_ref, send_ref, weights_ref, info_ref):
    @pl.when(pl.program_id(0) == 0)
    def _():
        scores = scores_ref[...]
        shifted = jnp.exp(scores - jnp.max(scores, axis=0, keepdims=True))
        weights = shifted / jnp.sum(shifted, axis=0, keepdims=True)
        weights_ref[...] = weights
        pick = pick_ref[...]
        entry = lax.broadcasted_iota(jnp.int32, (SLOTS, TOK), 0)
        placed = jnp.zeros((SLOTS, TOK), F32)
        for k in range(PICKS):
            placed = jnp.where(pick[k : k + 1] == entry, weights[k : k + 1], placed)
        owners = owners_ref[...].astype(F32)
        line = lax.broadcasted_iota(jnp.int32, (8, TOK), 0)
        named = jnp.zeros((8, TOK), F32)
        for c in range(CANDS):
            named = jnp.where(line == c, owners[c : c + 1], named)
        info_ref[...] = jnp.concatenate([placed, named], axis=0).astype(BF16)

    for b in range(MANY):
        for j in range(TILES):
            at = b * WIDE + j * L
            send_ref[b, j * L : (j + 1) * L, :] = jnp.transpose(cotangent_ref[:, at : at + L])
        send_ref[b, WIDE:, :] = info_ref[...]


def load_info(batch_ref, first=0):
    info = jnp.concatenate([batch_ref[first + i, WIDE:, :] for i in range(STEP)], axis=1).astype(F32)
    placed = [info[c * ROWS : (c + 1) * ROWS] for c in range(CANDS)]
    named = [
        jnp.broadcast_to(info[SLOTS + c : SLOTS + c + 1], (ROWS, STEP * TOK)) for c in range(CANDS)
    ]
    return placed, named


def place(placed, named):
    blocks = []
    for o in range(OWNERS):
        block = jnp.zeros((ROWS, STEP * TOK), F32)
        for c in range(CANDS):
            block = jnp.where(named[c] == float(o), placed[c], block)
        blocks.append(block.astype(BF16))
    return jnp.concatenate(blocks, axis=0)


def load_table(table_ref):
    return jnp.concatenate(
        [table_ref[:, j * ROWS : (j + 1) * ROWS, :].reshape(TABLE, L) for j in range(TILES)], axis=1
    )


def load_cotangent(batch_ref, first):
    return jnp.concatenate([batch_ref[first + i, :WIDE, :] for i in range(STEP)], axis=1).astype(F32)


def forward_kernel(batch_ref, table_ref, gain_ref, memory_ref, sums_ref, placed_ref):
    turned = jnp.transpose(load_table(table_ref))
    gain = gain_ref[...]
    for first in range(0, GROUP, STEP):
        at = slice(first * TOK, (first + STEP) * TOK)
        placed = place(*load_info(batch_ref, first))
        placed_ref[:, at] = placed
        memory = dot(turned, placed, ((1,), (0,)))
        memory_ref[:, at] = memory
        scaled = load_cotangent(batch_ref, first) * gain
        square = jnp.sum(memory * memory, axis=0, keepdims=True)
        cross = jnp.sum(scaled * memory, axis=0, keepdims=True)
        both = jnp.concatenate([square, cross], axis=0)
        for g in range(sums_ref.shape[0]):
            sums_ref[g, :, at] = both


def split(value):
    high = value.astype(BF16).astype(F32)
    return high, value - high


def gain_rows(rows):
    high, low = split(rows)
    return jnp.concatenate([high, low, jnp.zeros((8 - 2 * TILES, L), F32)], axis=0).astype(BF16)


def backward_kernel(
    batch_ref, gain_ref, memory_ref, sums_ref, placed_ref, out_ref, grad_ref, send_ref, out_held, grad_held, sems
):
    gain = gain_ref[...]
    gain_sum = jnp.zeros((WIDE, L), F32)
    for first in range(0, GROUP, STEP):
        at = slice(first * TOK, (first + STEP) * TOK)
        sums = jnp.sum(sums_ref[:, :, at], axis=0)
        inverse = lax.rsqrt(sums[0:1] / D + norm_epsilon)
        factor = inverse * inverse * inverse * (sums[1:2] / D)
        memory = memory_ref[:, at]
        cotangent = load_cotangent(batch_ref, first)
        normed = memory * inverse
        out_held[:, at] = (normed * gain).astype(BF16)
        grad_held[:, at] = (inverse * (cotangent * gain) - memory * factor).astype(BF16)
        gain_part = cotangent * normed
        gain_sum += sum(gain_part[:, i * L : (i + 1) * L] for i in range(STEP))
    out_copy = pltpu.make_async_copy(out_held, out_ref, sems.at[0])
    grad_copy = pltpu.make_async_copy(grad_held, grad_ref, sems.at[1])
    out_copy.start()
    grad_copy.start()
    total = dot(placed_ref[...], grad_held[...], ((1,), (1,))).astype(BF16)
    for j in range(TILES):
        send_ref[:, j * ROWS : (j + 1) * ROWS, :] = total[:, j * L : (j + 1) * L].reshape(OWNERS, ROWS, L)
    turned = jnp.transpose(gain_sum)
    rows = [jnp.sum(turned[:, j * L : (j + 1) * L], axis=0, keepdims=True) for j in range(TILES)]
    tail = gain_rows(jnp.concatenate(rows, axis=0))
    for o in range(OWNERS):
        send_ref[o, GAIN_AT:, :] = tail
    out_copy.wait()
    grad_copy.wait()


def placed_grad_kernel(batch_ref, table_ref, out_ref, grad_ref, send_ref):
    _, named = load_info(batch_ref)
    full = dot(load_table(table_ref), grad_ref[...], ((1,), (0,)))
    found = [jnp.zeros((ROWS, STEP * TOK), F32) for _ in range(CANDS)]
    for o in range(OWNERS):
        block = full[o * ROWS : (o + 1) * ROWS]
        for c in range(CANDS):
            found[c] = jnp.where(named[c] == float(o), block, found[c])
    for i in range(STEP):
        send_ref[i, :WIDE, :] = out_ref[:, i * TOK : (i + 1) * TOK]
        for c in range(CANDS):
            send_ref[i, WIDE + c * ROWS : WIDE + (c + 1) * ROWS, :] = found[c][
                :, i * TOK : (i + 1) * TOK
            ].astype(BF16)


def merge(parts):
    total = jnp.sum(parts, axis=0)
    gain = total[GAIN_AT : GAIN_AT + TILES] + total[GAIN_AT + TILES : GAIN_AT + 2 * TILES]
    return total[:GAIN_AT], gain


def plane_kernel(parts_ref, send_ref):
    for b in range(parts_ref.shape[1]):
        rows, gain = merge(parts_ref[:, b].astype(F32))
        send_ref[b, :GAIN_AT, :] = rows.astype(BF16)
        send_ref[b, GAIN_AT:, :] = gain_rows(gain)


def share_kernel(parts_ref, send_ref):
    rows, gain = merge(parts_ref[...].astype(F32))
    send_ref[:GAIN_AT, :] = rows.astype(BF16)
    send_ref[GAIN_AT:, :] = gain_rows(gain)


def adam_kernel(grad_ref, table_ref, first_ref, second_ref, new_table_ref, new_first_ref, new_second_ref, gain_ref):
    for b in range(grad_ref.shape[0]):
        tail = grad_ref[b, GAIN_AT:, :].astype(F32)
        for j in range(TILES):
            at = b * WIDE + j * L
            grad = grad_ref[b, j * ROWS : (j + 1) * ROWS, :].astype(F32)
            first = beta_first * first_ref[:, at : at + L] + (1.0 - beta_first) * grad
            second = beta_second * second_ref[:, at : at + L] + (1.0 - beta_second) * grad * grad
            update = learning_rate * (first / first_bias) / (jnp.sqrt(second / second_bias) + adam_epsilon)
            new_first_ref[:, at : at + L] = first
            new_second_ref[:, at : at + L] = second
            new_table_ref[:, at : at + L] = (table_ref[:, at : at + L].astype(F32) - update).astype(BF16)
            gain_ref[:, at : at + L] = tail[j : j + 1] + tail[TILES + j : TILES + j + 1]


def out_kernel(parts_ref, pick_ref, weights_ref, out_ref, score_ref, placed_grad_ref):
    step = pl.program_id(0)
    for b in range(MANY):
        for j in range(TILES):
            at = b * WIDE + j * L
            out_ref[:, at : at + L] = jnp.transpose(parts_ref[b, j * L : (j + 1) * L, :])
    part = sum(parts_ref[b, WIDE:, :].astype(F32) for b in range(MANY))

    @pl.when(step == 0)
    def _():
        placed_grad_ref[...] = part

    @pl.when(step > 0)
    def _():
        placed_grad_ref[...] += part

    @pl.when(step == pl.num_programs(0) - 1)
    def _():
        pick = pick_ref[...]
        weights = weights_ref[...]
        weight_grad = jnp.zeros((PICKS, TOK), F32)
        for m in range(SLOTS):
            weight_grad = jnp.where(pick == m, placed_grad_ref[m : m + 1, :], weight_grad)
        mean = jnp.sum(weights * weight_grad, axis=0, keepdims=True)
        score_ref[...] = weights * (weight_grad - mean)


def last_kernel(
    parts_ref, pick_ref, weights_ref, grad_ref, table_ref, first_ref, second_ref,
    out_ref, score_ref, new_table_ref, new_first_ref, new_second_ref, gain_ref, placed_grad_ref,
):
    adam_kernel(grad_ref, table_ref, first_ref, second_ref, new_table_ref, new_first_ref, new_second_ref, gain_ref)
    out_kernel(parts_ref, pick_ref, weights_ref, out_ref, score_ref, placed_grad_ref)


def exchange(array, axes):
    return lax.all_to_all(array, axes, split_axis=0, concat_axis=0, tiled=True)


def per_device(
    owners,
    pick_index,
    key_scores,
    output_cotangent,
    value_table,
    first_moment,
    second_moment,
    norm_gain,
):
    groups = lax.axis_size("xh")
    steps = GROUP // STEP
    block_index = lax.axis_index(TEAM)

    whole = lambda *dims: pl.BlockSpec(dims, lambda i: (0,) * len(dims))

    table_send = pl.pallas_call(
        table_kernel,
        out_shape=in_hbm(groups, GROUP, TILES * ROWS, L, BF16),
        compiler_params=PARAMS,
        name="table_send",
    )(value_table)
    table = exchange(table_send.reshape(OWNERS, TILES * ROWS, L), PLANE)

    batch_send, weights = pl.pallas_call(
        pack_kernel,
        grid=(GROUP // MANY,),
        in_specs=[
            whole(CANDS, TOK),
            whole(PICKS, TOK),
            whole(PICKS, TOK),
            pl.BlockSpec((TOK, MANY * WIDE), lambda i: (0, i)),
        ],
        out_specs=[pl.BlockSpec((MANY, WIDE + INFO, L), lambda i: (i, 0, 0)), whole(PICKS, TOK)],
        out_shape=(in_hbm(GROUP, WIDE + INFO, L, BF16), shape(PICKS, TOK, F32)),
        scratch_shapes=[pltpu.VMEM((INFO, TOK), BF16)],
        compiler_params=PARAMS,
        name="pack",
    )(owners.T, pick_index.T, key_scores.T, output_cotangent)
    batch = exchange(batch_send, TEAM)
    gain = lax.dynamic_slice(norm_gain, (block_index * WIDE,), (WIDE,)).reshape(WIDE, 1)

    batch_spec = pl.BlockSpec((STEP, WIDE + INFO, L), lambda i: (i, 0, 0))
    table_spec = whole(OWNERS, TILES * ROWS, L)
    wide_spec = pl.BlockSpec((WIDE, STEP * TOK), lambda i: (0, i))
    sums_spec = pl.BlockSpec((GROUP, 2, STEP * TOK), lambda i: (0, 0, i))
    tokens = GROUP * TOK

    vmem = pl.BlockSpec(memory_space=pltpu.VMEM)
    hbm = pl.BlockSpec(memory_space=pl.ANY)
    memory, sums_send, placed = pl.pallas_call(
        forward_kernel,
        in_specs=[vmem] * 3,
        out_specs=[vmem] * 3,
        out_shape=(
            shape(WIDE, tokens, F32),
            shape(GROUP, 2, tokens, F32),
            shape(TABLE, tokens, BF16),
        ),
        compiler_params=PARAMS,
        name="forward",
    )(batch, table, gain)
    sums = exchange(sums_send, TEAM)

    out_turned, memory_grad, grad_send = pl.pallas_call(
        backward_kernel,
        in_specs=[vmem] * 5,
        out_specs=[hbm, hbm, pl.BlockSpec()],
        out_shape=(
            in_hbm(WIDE, tokens, BF16),
            in_hbm(WIDE, tokens, BF16),
            in_hbm(OWNERS, GRAD, L, BF16),
        ),
        scratch_shapes=[
            pltpu.VMEM((WIDE, tokens), BF16),
            pltpu.VMEM((WIDE, tokens), BF16),
            pltpu.SemaphoreType.DMA((2,)),
        ],
        compiler_params=PARAMS,
        name="backward",
    )(batch, gain, memory, sums, placed)
    plane_parts = exchange(grad_send, PLANE)

    back_send = pl.pallas_call(
        placed_grad_kernel,
        grid=(steps,),
        in_specs=[batch_spec, table_spec, wide_spec, wide_spec],
        out_specs=pl.BlockSpec((STEP, BACK, L), lambda i: (i, 0, 0)),
        out_shape=in_hbm(GROUP, BACK, L, BF16),
        compiler_params=PARAMS,
        name="placed_grad",
    )(batch, table, out_turned, memory_grad)

    plane_parts, back_send = lax.optimization_barrier((plane_parts, back_send))
    shares_send = pl.pallas_call(
        plane_kernel,
        out_shape=shape(GROUP, GRAD, L, BF16),
        compiler_params=PARAMS,
        name="plane_sum",
    )(plane_parts.reshape(groups, GROUP, GRAD, L))
    shares = exchange(shares_send, "dp")
    total = pl.pallas_call(
        share_kernel,
        out_shape=shape(GRAD, L, BF16),
        compiler_params=PARAMS,
        name="share_sum",
    )(shares)
    total, back_send = lax.optimization_barrier((total, back_send))
    totals = lax.all_gather(total, "dp", axis=0, tiled=False)

    back = exchange(back_send, TEAM)
    rows_spec = pl.BlockSpec((ROWS, MANY * WIDE), lambda i: (0, i))
    memory_out, score_turned, new_table, new_first, new_second, gain_gradient = pl.pallas_call(
        last_kernel,
        grid=(GROUP // MANY,),
        in_specs=[
            pl.BlockSpec((MANY, BACK, L), lambda i: (i, 0, 0)),
            whole(PICKS, TOK),
            whole(PICKS, TOK),
            pl.BlockSpec((MANY, GRAD, L), lambda i: (i, 0, 0)),
            rows_spec,
            rows_spec,
            rows_spec,
        ],
        out_specs=[
            pl.BlockSpec((TOK, MANY * WIDE), lambda i: (0, i)),
            whole(PICKS, TOK),
            rows_spec,
            rows_spec,
            rows_spec,
            pl.BlockSpec((1, MANY * WIDE), lambda i: (0, i)),
        ],
        out_shape=(
            shape(TOK, D, BF16),
            shape(PICKS, TOK, F32),
            shape(ROWS, D, BF16),
            shape(ROWS, D, F32),
            shape(ROWS, D, F32),
            shape(1, D, F32),
        ),
        scratch_shapes=[pltpu.VMEM((SLOTS, TOK), F32)],
        compiler_params=PARAMS,
        name="last",
    )(back, pick_index.T, weights, totals, value_table, first_moment, second_moment)
    return (memory_out, score_turned.T, gain_gradient.reshape(D), new_table, new_first, new_second)


def solution(mesh):
    planes, mem_count = mesh.shape["dp"], mesh.shape["mem"]
    split_mesh = Mesh(mesh.devices.reshape(planes, mem_count // GROUP, PAIR, RING), ("dp",) + PLANE)
    tokens = P(("dp",) + PLANE, None)
    rows = P(PLANE, None)
    return jax.shard_map(
        per_device,
        mesh=split_mesh,
        in_specs=(tokens, tokens, tokens, tokens, rows, rows, rows, P()),
        out_specs=(tokens, tokens, P(), rows, rows, rows),
        check_vma=False,
    )
```

```python
import functools

import jax
import jax.numpy as jnp
from jax import lax
from jax.experimental import pallas as pl
from jax.experimental.pallas import tpu as pltpu
from jax.sharding import Mesh
from jax.sharding import PartitionSpec as P

beta_first = 0.9
beta_second = 0.95
learning_rate = 0.01
adam_epsilon = 1e-08
first_bias = 1.0 - (0.9**50) ** 2
second_bias = 1.0 - (0.95**50) ** 2
norm_epsilon = 1e-05

L = 128
PAIR = 2
RING = 8
GROUP = PAIR * RING
CANDS = 3
ROWS = 32
PICKS = 32
D = 4096
WIDE = D // GROUP
TILES = WIDE // L
TOK = 128
SLOTS = CANDS * ROWS
TABLE = 1024
OWNERS = TABLE // ROWS
INFO = SLOTS + 8
GAIN_AT = TILES * ROWS
GRAD = GAIN_AT + 8
BACK = WIDE + SLOTS
STEP = 4
MANY = 4
LAST = 8
PLANE = ("xh", "xl", "yc")
TEAM = ("xl", "yc")
VMEM_LIMIT = 32 * 1024 * 1024
F32 = jnp.float32
BF16 = jnp.bfloat16
PARAMS = pltpu.CompilerParams(vmem_limit_bytes=VMEM_LIMIT)


def dot(a, b, dims):
    return lax.dot_general(a, b, (dims, ((), ())), preferred_element_type=F32)


def shape(*dims_and_type):
    return jax.ShapeDtypeStruct(dims_and_type[:-1], dims_and_type[-1])


def in_hbm(*dims_and_type):
    return pltpu.HBM(dims_and_type[:-1], dims_and_type[-1])


def table_kernel(table_ref, out_ref, sems):
    copies = []
    for x in range(out_ref.shape[0]):
        for b in range(GROUP):
            for j in range(TILES):
                source = table_ref.at[:, pl.ds(b * WIDE + j * L, L)]
                target = out_ref.at[x, b, pl.ds(j * ROWS, ROWS), :]
                copies.append(pltpu.make_async_copy(source, target, sems.at[len(copies)]))
    for copy in copies:
        copy.start()
    for copy in copies:
        copy.wait()


def turn_kernel(table_ref, out_ref):
    out_ref[...] = jnp.transpose(load_table(table_ref))


def pack_kernel(owners_ref, pick_ref, scores_ref, cotangent_ref, send_ref, weights_ref, info_ref):
    @pl.when(pl.program_id(0) == 0)
    def _():
        scores = scores_ref[...]
        shifted = jnp.exp(scores - jnp.max(scores, axis=0, keepdims=True))
        weights = shifted / jnp.sum(shifted, axis=0, keepdims=True)
        weights_ref[...] = weights
        pick = pick_ref[...]
        entry = lax.broadcasted_iota(jnp.int32, (SLOTS, TOK), 0)
        placed = jnp.zeros((SLOTS, TOK), F32)
        for k in range(PICKS):
            placed = jnp.where(pick[k : k + 1] == entry, weights[k : k + 1], placed)
        owners = owners_ref[...].astype(F32)
        line = lax.broadcasted_iota(jnp.int32, (8, TOK), 0)
        named = jnp.zeros((8, TOK), F32)
        for c in range(CANDS):
            named = jnp.where(line == c, owners[c : c + 1], named)
        info_ref[...] = jnp.concatenate([placed, named], axis=0).astype(BF16)

    for b in range(MANY):
        for j in range(TILES):
            at = b * WIDE + j * L
            send_ref[b, j * L : (j + 1) * L, :] = jnp.transpose(cotangent_ref[:, at : at + L])
        send_ref[b, WIDE:, :] = info_ref[...]


def load_info(batch_ref, first=0):
    info = jnp.concatenate([batch_ref[first + i, WIDE:, :] for i in range(STEP)], axis=1).astype(F32)
    placed = [info[c * ROWS : (c + 1) * ROWS] for c in range(CANDS)]
    named = [
        jnp.broadcast_to(info[SLOTS + c : SLOTS + c + 1], (ROWS, STEP * TOK)) for c in range(CANDS)
    ]
    return placed, named


def place(placed, named):
    blocks = []
    for o in range(OWNERS):
        block = jnp.zeros((ROWS, STEP * TOK), F32)
        for c in range(CANDS):
            block = jnp.where(named[c] == float(o), placed[c], block)
        blocks.append(block.astype(BF16))
    return jnp.concatenate(blocks, axis=0)


def load_table(table_ref):
    return jnp.concatenate(
        [table_ref[:, j * ROWS : (j + 1) * ROWS, :].reshape(TABLE, L) for j in range(TILES)], axis=1
    )


def load_cotangent(batch_ref, first):
    return jnp.concatenate([batch_ref[first + i, :WIDE, :] for i in range(STEP)], axis=1).astype(F32)


def forward_kernel(batch_ref, turned_ref, gain_ref, memory_ref, sums_ref, placed_ref):
    turned = turned_ref[...]
    gain = gain_ref[...]
    for first in range(0, GROUP, STEP):
        at = slice(first * TOK, (first + STEP) * TOK)
        placed = place(*load_info(batch_ref, first))
        placed_ref[:, at] = placed
        memory = dot(turned, placed, ((1,), (0,)))
        memory_ref[:, at] = memory
        scaled = load_cotangent(batch_ref, first) * gain
        square = jnp.sum(memory * memory, axis=0, keepdims=True)
        cross = jnp.sum(scaled * memory, axis=0, keepdims=True)
        both = jnp.concatenate([square, cross], axis=0)
        for g in range(sums_ref.shape[0]):
            sums_ref[g, :, at] = both


def split(value):
    high = value.astype(BF16).astype(F32)
    return high, value - high


def gain_rows(rows):
    high, low = split(rows)
    return jnp.concatenate([high, low, jnp.zeros((8 - 2 * TILES, L), F32)], axis=0).astype(BF16)


def backward_kernel(
    batch_ref, gain_ref, memory_ref, sums_ref, placed_ref, out_ref, grad_ref, send_ref, out_held, grad_held, sems
):
    gain = gain_ref[...]
    gain_sum = jnp.zeros((WIDE, L), F32)
    for first in range(0, GROUP, STEP):
        at = slice(first * TOK, (first + STEP) * TOK)
        sums = jnp.sum(sums_ref[:, :, at], axis=0)
        inverse = lax.rsqrt(sums[0:1] / D + norm_epsilon)
        factor = inverse * inverse * inverse * (sums[1:2] / D)
        memory = memory_ref[:, at]
        cotangent = load_cotangent(batch_ref, first)
        normed = memory * inverse
        out_held[:, at] = (normed * gain).astype(BF16)
        grad_held[:, at] = (inverse * (cotangent * gain) - memory * factor).astype(BF16)
        gain_part = cotangent * normed
        gain_sum += sum(gain_part[:, i * L : (i + 1) * L] for i in range(STEP))
    out_copy = pltpu.make_async_copy(out_held, out_ref, sems.at[0])
    grad_copy = pltpu.make_async_copy(grad_held, grad_ref, sems.at[1])
    out_copy.start()
    grad_copy.start()
    total = dot(placed_ref[...], grad_held[...], ((1,), (1,))).astype(BF16)
    for j in range(TILES):
        send_ref[:, j * ROWS : (j + 1) * ROWS, :] = total[:, j * L : (j + 1) * L].reshape(OWNERS, ROWS, L)
    turned = jnp.transpose(gain_sum)
    rows = [jnp.sum(turned[:, j * L : (j + 1) * L], axis=0, keepdims=True) for j in range(TILES)]
    tail = gain_rows(jnp.concatenate(rows, axis=0))
    for o in range(OWNERS):
        send_ref[o, GAIN_AT:, :] = tail
    out_copy.wait()
    grad_copy.wait()


def placed_grad_kernel(batch_ref, table_ref, out_ref, grad_ref, send_ref):
    _, named = load_info(batch_ref)
    full = dot(load_table(table_ref), grad_ref[...], ((1,), (0,)))
    found = [jnp.zeros((ROWS, STEP * TOK), F32) for _ in range(CANDS)]
    for o in range(OWNERS):
        block = full[o * ROWS : (o + 1) * ROWS]
        for c in range(CANDS):
            found[c] = jnp.where(named[c] == float(o), block, found[c])
    for i in range(STEP):
        send_ref[i, :WIDE, :] = out_ref[:, i * TOK : (i + 1) * TOK]
        for c in range(CANDS):
            send_ref[i, WIDE + c * ROWS : WIDE + (c + 1) * ROWS, :] = found[c][
                :, i * TOK : (i + 1) * TOK
            ].astype(BF16)


def merge(parts):
    total = jnp.sum(parts, axis=0)
    gain = total[GAIN_AT : GAIN_AT + TILES] + total[GAIN_AT + TILES : GAIN_AT + 2 * TILES]
    return total[:GAIN_AT], gain


def plane_kernel(parts_ref, send_ref):
    for b in range(parts_ref.shape[1]):
        rows, gain = merge(parts_ref[:, b].astype(F32))
        send_ref[b, :GAIN_AT, :] = rows.astype(BF16)
        send_ref[b, GAIN_AT:, :] = gain_rows(gain)


def share_kernel(parts_ref, send_ref):
    rows, gain = merge(parts_ref[...].astype(F32))
    send_ref[:GAIN_AT, :] = rows.astype(BF16)
    send_ref[GAIN_AT:, :] = gain_rows(gain)


def adam_kernel(grad_ref, table_ref, first_ref, second_ref, new_table_ref, new_first_ref, new_second_ref, gain_ref):
    for b in range(grad_ref.shape[0]):
        tail = grad_ref[b, GAIN_AT:, :].astype(F32)
        for j in range(TILES):
            at = b * WIDE + j * L
            grad = grad_ref[b, j * ROWS : (j + 1) * ROWS, :].astype(F32)
            first = beta_first * first_ref[:, at : at + L] + (1.0 - beta_first) * grad
            second = beta_second * second_ref[:, at : at + L] + (1.0 - beta_second) * grad * grad
            update = learning_rate * (first / first_bias) / (jnp.sqrt(second / second_bias) + adam_epsilon)
            new_first_ref[:, at : at + L] = first
            new_second_ref[:, at : at + L] = second
            new_table_ref[:, at : at + L] = (table_ref[:, at : at + L].astype(F32) - update).astype(BF16)
            gain_ref[:, at : at + L] = tail[j : j + 1] + tail[TILES + j : TILES + j + 1]


def out_kernel(parts_ref, pick_ref, weights_ref, out_ref, score_ref, placed_grad_ref):
    step = pl.program_id(0)
    for b in range(LAST):
        for j in range(TILES):
            at = b * WIDE + j * L
            out_ref[:, at : at + L] = jnp.transpose(parts_ref[b, j * L : (j + 1) * L, :])
    part = sum(parts_ref[b, WIDE:, :].astype(F32) for b in range(LAST))

    @pl.when(step == 0)
    def _():
        placed_grad_ref[...] = part

    @pl.when(step > 0)
    def _():
        placed_grad_ref[...] += part

    @pl.when(step == pl.num_programs(0) - 1)
    def _():
        pick = pick_ref[...]
        weights = weights_ref[...]
        weight_grad = jnp.zeros((PICKS, TOK), F32)
        for m in range(SLOTS):
            weight_grad = jnp.where(pick == m, placed_grad_ref[m : m + 1, :], weight_grad)
        mean = jnp.sum(weights * weight_grad, axis=0, keepdims=True)
        score_ref[...] = weights * (weight_grad - mean)


def last_kernel(
    parts_ref, pick_ref, weights_ref, grad_ref, table_ref, first_ref, second_ref,
    out_ref, score_ref, new_table_ref, new_first_ref, new_second_ref, gain_ref, placed_grad_ref,
):
    adam_kernel(grad_ref, table_ref, first_ref, second_ref, new_table_ref, new_first_ref, new_second_ref, gain_ref)
    out_kernel(parts_ref, pick_ref, weights_ref, out_ref, score_ref, placed_grad_ref)


def exchange(array, axes):
    return lax.all_to_all(array, axes, split_axis=0, concat_axis=0, tiled=True)


def per_device(
    owners,
    pick_index,
    key_scores,
    output_cotangent,
    value_table,
    first_moment,
    second_moment,
    norm_gain,
):
    groups = lax.axis_size("xh")
    steps = GROUP // STEP
    block_index = lax.axis_index(TEAM)

    whole = lambda *dims: pl.BlockSpec(dims, lambda i: (0,) * len(dims))

    table_send = pl.pallas_call(
        table_kernel,
        in_specs=[pl.BlockSpec(memory_space=pltpu.HBM)],
        out_specs=pl.BlockSpec(memory_space=pltpu.HBM),
        out_shape=in_hbm(groups, GROUP, TILES * ROWS, L, BF16),
        scratch_shapes=[pltpu.SemaphoreType.DMA((groups * GROUP * TILES,))],
        compiler_params=PARAMS,
        name="table_send",
    )(pltpu.with_memory_space_constraint(value_table, pltpu.HBM))
    table = exchange(table_send.reshape(OWNERS, TILES * ROWS, L), PLANE)

    batch_send, weights = pl.pallas_call(
        pack_kernel,
        grid=(GROUP // MANY,),
        in_specs=[
            whole(CANDS, TOK),
            whole(PICKS, TOK),
            whole(PICKS, TOK),
            pl.BlockSpec((TOK, MANY * WIDE), lambda i: (0, i)),
        ],
        out_specs=[pl.BlockSpec((MANY, WIDE + INFO, L), lambda i: (i, 0, 0)), whole(PICKS, TOK)],
        out_shape=(in_hbm(GROUP, WIDE + INFO, L, BF16), shape(PICKS, TOK, F32)),
        scratch_shapes=[pltpu.VMEM((INFO, TOK), BF16)],
        compiler_params=PARAMS,
        name="pack",
    )(owners.T, pick_index.T, key_scores.T, output_cotangent)
    batch = exchange(batch_send, TEAM)
    gain = lax.dynamic_slice(norm_gain, (block_index * WIDE,), (WIDE,)).reshape(WIDE, 1)

    batch_spec = pl.BlockSpec((STEP, WIDE + INFO, L), lambda i: (i, 0, 0))
    table_spec = whole(OWNERS, TILES * ROWS, L)
    wide_spec = pl.BlockSpec((WIDE, STEP * TOK), lambda i: (0, i))
    sums_spec = pl.BlockSpec((GROUP, 2, STEP * TOK), lambda i: (0, 0, i))
    tokens = GROUP * TOK

    vmem = pl.BlockSpec(memory_space=pltpu.VMEM)
    hbm = pl.BlockSpec(memory_space=pl.ANY)
    turned = pl.pallas_call(
        turn_kernel,
        in_specs=[vmem],
        out_specs=vmem,
        out_shape=shape(WIDE, TABLE, BF16),
        compiler_params=PARAMS,
        name="turn",
    )(table)
    memory, sums_send, placed = pl.pallas_call(
        forward_kernel,
        in_specs=[vmem] * 3,
        out_specs=[vmem] * 3,
        out_shape=(
            shape(WIDE, tokens, F32),
            shape(GROUP, 2, tokens, F32),
            shape(TABLE, tokens, BF16),
        ),
        compiler_params=PARAMS,
        name="forward",
    )(batch, turned, gain)
    sums = exchange(sums_send, TEAM)

    out_turned, memory_grad, grad_send = pl.pallas_call(
        backward_kernel,
        in_specs=[vmem] * 5,
        out_specs=[hbm, hbm, pl.BlockSpec()],
        out_shape=(
            in_hbm(WIDE, tokens, BF16),
            in_hbm(WIDE, tokens, BF16),
            in_hbm(OWNERS, GRAD, L, BF16),
        ),
        scratch_shapes=[
            pltpu.VMEM((WIDE, tokens), BF16),
            pltpu.VMEM((WIDE, tokens), BF16),
            pltpu.SemaphoreType.DMA((2,)),
        ],
        compiler_params=PARAMS,
        name="backward",
    )(batch, gain, memory, sums, placed)
    plane_parts = exchange(grad_send, PLANE)

    back_send = pl.pallas_call(
        placed_grad_kernel,
        grid=(steps,),
        in_specs=[batch_spec, table_spec, wide_spec, wide_spec],
        out_specs=pl.BlockSpec((STEP, BACK, L), lambda i: (i, 0, 0)),
        out_shape=in_hbm(GROUP, BACK, L, BF16),
        compiler_params=PARAMS,
        name="placed_grad",
    )(batch, table, out_turned, memory_grad)

    plane_parts, back_send = lax.optimization_barrier((plane_parts, back_send))
    shares_send = pl.pallas_call(
        plane_kernel,
        out_shape=shape(GROUP, GRAD, L, BF16),
        compiler_params=PARAMS,
        name="plane_sum",
    )(plane_parts.reshape(groups, GROUP, GRAD, L))
    shares = exchange(shares_send, "dp")
    total = pl.pallas_call(
        share_kernel,
        out_shape=shape(GRAD, L, BF16),
        compiler_params=PARAMS,
        name="share_sum",
    )(shares)
    total, back_send = lax.optimization_barrier((total, back_send))
    totals = lax.all_gather(total, "dp", axis=0, tiled=False)

    back = exchange(back_send, TEAM)
    rows_spec = pl.BlockSpec((ROWS, LAST * WIDE), lambda i: (0, i))
    memory_out, score_turned, new_table, new_first, new_second, gain_gradient = pl.pallas_call(
        last_kernel,
        grid=(GROUP // LAST,),
        in_specs=[
            pl.BlockSpec((LAST, BACK, L), lambda i: (i, 0, 0)),
            whole(PICKS, TOK),
            whole(PICKS, TOK),
            pl.BlockSpec((LAST, GRAD, L), lambda i: (i, 0, 0)),
            rows_spec,
            rows_spec,
            rows_spec,
        ],
        out_specs=[
            pl.BlockSpec((TOK, LAST * WIDE), lambda i: (0, i)),
            whole(PICKS, TOK),
            rows_spec,
            rows_spec,
            rows_spec,
            pl.BlockSpec((1, LAST * WIDE), lambda i: (0, i)),
        ],
        out_shape=(
            shape(TOK, D, BF16),
            shape(PICKS, TOK, F32),
            shape(ROWS, D, BF16),
            shape(ROWS, D, F32),
            shape(ROWS, D, F32),
            shape(1, D, F32),
        ),
        scratch_shapes=[pltpu.VMEM((SLOTS, TOK), F32)],
        compiler_params=PARAMS,
        name="last",
    )(back, pick_index.T, weights, totals, value_table, first_moment, second_moment)
    return (memory_out, score_turned.T, gain_gradient.reshape(D), new_table, new_first, new_second)


def solution(mesh):
    planes, mem_count = mesh.shape["dp"], mesh.shape["mem"]
    split_mesh = Mesh(mesh.devices.reshape(planes, mem_count // GROUP, PAIR, RING), ("dp",) + PLANE)
    tokens = P(("dp",) + PLANE, None)
    rows = P(PLANE, None)
    return jax.shard_map(
        per_device,
        mesh=split_mesh,
        in_specs=(tokens, tokens, tokens, tokens, rows, rows, rows, P()),
        out_specs=(tokens, tokens, P(), rows, rows, rows),
        check_vma=False,
    )
```

```python
import functools

import jax
import jax.numpy as jnp
from jax import lax
from jax.experimental import pallas as pl
from jax.experimental.pallas import tpu as pltpu
from jax.sharding import Mesh
from jax.sharding import PartitionSpec as P

beta_first = 0.9
beta_second = 0.95
learning_rate = 0.01
adam_epsilon = 1e-08
first_bias = 1.0 - (0.9**50) ** 2
second_bias = 1.0 - (0.95**50) ** 2
norm_epsilon = 1e-05

L = 128
PAIR = 2
RING = 8
GROUP = PAIR * RING
CANDS = 3
ROWS = 32
PICKS = 32
D = 4096
WIDE = D // GROUP
TILES = WIDE // L
TOK = 128
SLOTS = CANDS * ROWS
TABLE = 1024
OWNERS = TABLE // ROWS
INFO = SLOTS + 8
GAIN_AT = TILES * ROWS
GRAD = GAIN_AT + 8
BACK = WIDE + SLOTS
STEP = 4
MANY = 4
LAST = 8
PLANE = ("xh", "xl", "yc")
TEAM = ("xl", "yc")
VMEM_LIMIT = 32 * 1024 * 1024
F32 = jnp.float32
BF16 = jnp.bfloat16
PARAMS = pltpu.CompilerParams(vmem_limit_bytes=VMEM_LIMIT)


def dot(a, b, dims):
    return lax.dot_general(a, b, (dims, ((), ())), preferred_element_type=F32)


def shape(*dims_and_type):
    return jax.ShapeDtypeStruct(dims_and_type[:-1], dims_and_type[-1])


def in_hbm(*dims_and_type):
    return pltpu.HBM(dims_and_type[:-1], dims_and_type[-1])


def table_kernel(table_ref, out_ref):
    for b in range(GROUP):
        for j in range(TILES):
            at = b * WIDE + j * L
            tile = table_ref[:, at : at + L]
            for x in range(out_ref.shape[0]):
                out_ref[x, b, j * ROWS : (j + 1) * ROWS, :] = tile


def turn_kernel(table_ref, out_ref):
    out_ref[...] = jnp.transpose(load_table(table_ref))


def pack_kernel(owners_ref, pick_ref, scores_ref, cotangent_ref, send_ref, weights_ref, info_ref):
    @pl.when(pl.program_id(0) == 0)
    def _():
        scores = scores_ref[...]
        shifted = jnp.exp(scores - jnp.max(scores, axis=0, keepdims=True))
        weights = shifted / jnp.sum(shifted, axis=0, keepdims=True)
        weights_ref[...] = weights
        pick = pick_ref[...]
        entry = lax.broadcasted_iota(jnp.int32, (SLOTS, TOK), 0)
        placed = jnp.zeros((SLOTS, TOK), F32)
        for k in range(PICKS):
            placed = jnp.where(pick[k : k + 1] == entry, weights[k : k + 1], placed)
        owners = owners_ref[...].astype(F32)
        line = lax.broadcasted_iota(jnp.int32, (8, TOK), 0)
        named = jnp.zeros((8, TOK), F32)
        for c in range(CANDS):
            named = jnp.where(line == c, owners[c : c + 1], named)
        info_ref[...] = jnp.concatenate([placed, named], axis=0).astype(BF16)

    for b in range(MANY):
        for j in range(TILES):
            at = b * WIDE + j * L
            send_ref[b, j * L : (j + 1) * L, :] = jnp.transpose(cotangent_ref[:, at : at + L])
        send_ref[b, WIDE:, :] = info_ref[...]


def load_info(batch_ref, first=0):
    info = jnp.concatenate([batch_ref[first + i, WIDE:, :] for i in range(STEP)], axis=1).astype(F32)
    placed = [info[c * ROWS : (c + 1) * ROWS] for c in range(CANDS)]
    named = [
        jnp.broadcast_to(info[SLOTS + c : SLOTS + c + 1], (ROWS, STEP * TOK)) for c in range(CANDS)
    ]
    return placed, named


def place(placed, named):
    blocks = []
    for o in range(OWNERS):
        block = jnp.zeros((ROWS, STEP * TOK), F32)
        for c in range(CANDS):
            block = jnp.where(named[c] == float(o), placed[c], block)
        blocks.append(block.astype(BF16))
    return jnp.concatenate(blocks, axis=0)


def load_table(table_ref):
    return jnp.concatenate(
        [table_ref[:, j * ROWS : (j + 1) * ROWS, :].reshape(TABLE, L) for j in range(TILES)], axis=1
    )


def load_cotangent(batch_ref, first):
    return jnp.concatenate([batch_ref[first + i, :WIDE, :] for i in range(STEP)], axis=1).astype(F32)


def forward_kernel(batch_ref, turned_ref, gain_ref, memory_ref, sums_ref, placed_ref):
    turned = turned_ref[...]
    gain = gain_ref[...]
    for first in range(0, GROUP, STEP):
        at = slice(first * TOK, (first + STEP) * TOK)
        placed = place(*load_info(batch_ref, first))
        placed_ref[:, at] = placed
        memory = dot(turned, placed, ((1,), (0,)))
        memory_ref[:, at] = memory
        scaled = load_cotangent(batch_ref, first) * gain
        square = jnp.sum(memory * memory, axis=0, keepdims=True)
        cross = jnp.sum(scaled * memory, axis=0, keepdims=True)
        both = jnp.concatenate([square, cross], axis=0)
        for g in range(sums_ref.shape[0]):
            sums_ref[g, :, at] = both


def split(value):
    high = value.astype(BF16).astype(F32)
    return high, value - high


def gain_rows(rows):
    high, low = split(rows)
    return jnp.concatenate([high, low, jnp.zeros((8 - 2 * TILES, L), F32)], axis=0).astype(BF16)


def backward_kernel(
    batch_ref, gain_ref, memory_ref, sums_ref, placed_ref, out_ref, grad_ref, send_ref, out_held, grad_held, sems
):
    gain = gain_ref[...]
    gain_sum = jnp.zeros((WIDE, L), F32)
    for first in range(0, GROUP, STEP):
        at = slice(first * TOK, (first + STEP) * TOK)
        sums = jnp.sum(sums_ref[:, :, at], axis=0)
        inverse = lax.rsqrt(sums[0:1] / D + norm_epsilon)
        factor = inverse * inverse * inverse * (sums[1:2] / D)
        memory = memory_ref[:, at]
        cotangent = load_cotangent(batch_ref, first)
        normed = memory * inverse
        out_held[:, at] = (normed * gain).astype(BF16)
        grad_held[:, at] = (inverse * (cotangent * gain) - memory * factor).astype(BF16)
        gain_part = cotangent * normed
        gain_sum += sum(gain_part[:, i * L : (i + 1) * L] for i in range(STEP))
    out_copy = pltpu.make_async_copy(out_held, out_ref, sems.at[0])
    grad_copy = pltpu.make_async_copy(grad_held, grad_ref, sems.at[1])
    out_copy.start()
    grad_copy.start()
    total = dot(placed_ref[...], grad_held[...], ((1,), (1,))).astype(BF16)
    for j in range(TILES):
        send_ref[:, j * ROWS : (j + 1) * ROWS, :] = total[:, j * L : (j + 1) * L].reshape(OWNERS, ROWS, L)
    turned = jnp.transpose(gain_sum)
    rows = [jnp.sum(turned[:, j * L : (j + 1) * L], axis=0, keepdims=True) for j in range(TILES)]
    tail = gain_rows(jnp.concatenate(rows, axis=0))
    for o in range(OWNERS):
        send_ref[o, GAIN_AT:, :] = tail
    out_copy.wait()
    grad_copy.wait()


def placed_grad_kernel(batch_ref, table_ref, out_ref, grad_ref, send_ref):
    _, named = load_info(batch_ref)
    full = dot(load_table(table_ref), grad_ref[...], ((1,), (0,)))
    found = [jnp.zeros((ROWS, STEP * TOK), F32) for _ in range(CANDS)]
    for o in range(OWNERS):
        block = full[o * ROWS : (o + 1) * ROWS]
        for c in range(CANDS):
            found[c] = jnp.where(named[c] == float(o), block, found[c])
    for i in range(STEP):
        send_ref[i, :WIDE, :] = out_ref[:, i * TOK : (i + 1) * TOK]
        for c in range(CANDS):
            send_ref[i, WIDE + c * ROWS : WIDE + (c + 1) * ROWS, :] = found[c][
                :, i * TOK : (i + 1) * TOK
            ].astype(BF16)


def merge(parts):
    total = jnp.sum(parts, axis=0)
    gain = total[GAIN_AT : GAIN_AT + TILES] + total[GAIN_AT + TILES : GAIN_AT + 2 * TILES]
    return total[:GAIN_AT], gain


def plane_kernel(parts_ref, send_ref):
    for b in range(parts_ref.shape[1]):
        rows, gain = merge(parts_ref[:, b].astype(F32))
        send_ref[b, :GAIN_AT, :] = rows.astype(BF16)
        send_ref[b, GAIN_AT:, :] = gain_rows(gain)


def share_kernel(parts_ref, send_ref):
    rows, gain = merge(parts_ref[...].astype(F32))
    send_ref[:GAIN_AT, :] = rows.astype(BF16)
    send_ref[GAIN_AT:, :] = gain_rows(gain)


def adam_kernel(grad_ref, table_ref, first_ref, second_ref, new_table_ref, new_first_ref, new_second_ref, gain_ref):
    for b in range(grad_ref.shape[0]):
        tail = grad_ref[b, GAIN_AT:, :].astype(F32)
        for j in range(TILES):
            at = b * WIDE + j * L
            grad = grad_ref[b, j * ROWS : (j + 1) * ROWS, :].astype(F32)
            first = beta_first * first_ref[:, at : at + L] + (1.0 - beta_first) * grad
            second = beta_second * second_ref[:, at : at + L] + (1.0 - beta_second) * grad * grad
            update = learning_rate * (first / first_bias) / (jnp.sqrt(second / second_bias) + adam_epsilon)
            new_first_ref[:, at : at + L] = first
            new_second_ref[:, at : at + L] = second
            new_table_ref[:, at : at + L] = (table_ref[:, at : at + L].astype(F32) - update).astype(BF16)
            gain_ref[:, at : at + L] = tail[j : j + 1] + tail[TILES + j : TILES + j + 1]


def out_kernel(parts_ref, pick_ref, weights_ref, out_ref, score_ref, placed_grad_ref):
    step = pl.program_id(0)
    for b in range(LAST):
        for j in range(TILES):
            at = b * WIDE + j * L
            out_ref[:, at : at + L] = jnp.transpose(parts_ref[b, j * L : (j + 1) * L, :])
    part = sum(parts_ref[b, WIDE:, :].astype(F32) for b in range(LAST))

    @pl.when(step == 0)
    def _():
        placed_grad_ref[...] = part

    @pl.when(step > 0)
    def _():
        placed_grad_ref[...] += part

    @pl.when(step == pl.num_programs(0) - 1)
    def _():
        pick = pick_ref[...]
        weights = weights_ref[...]
        weight_grad = jnp.zeros((PICKS, TOK), F32)
        for m in range(SLOTS):
            weight_grad = jnp.where(pick == m, placed_grad_ref[m : m + 1, :], weight_grad)
        mean = jnp.sum(weights * weight_grad, axis=0, keepdims=True)
        score_ref[...] = weights * (weight_grad - mean)


def last_kernel(
    parts_ref, pick_ref, weights_ref, grad_ref, table_ref, first_ref, second_ref,
    out_ref, score_ref, new_table_ref, new_first_ref, new_second_ref, gain_ref, placed_grad_ref,
):
    adam_kernel(grad_ref, table_ref, first_ref, second_ref, new_table_ref, new_first_ref, new_second_ref, gain_ref)
    out_kernel(parts_ref, pick_ref, weights_ref, out_ref, score_ref, placed_grad_ref)


def exchange(array, axes):
    return lax.all_to_all(array, axes, split_axis=0, concat_axis=0, tiled=True)


def per_device(
    owners,
    pick_index,
    key_scores,
    output_cotangent,
    value_table,
    first_moment,
    second_moment,
    norm_gain,
):
    groups = lax.axis_size("xh")
    steps = GROUP // STEP
    block_index = lax.axis_index(TEAM)

    whole = lambda *dims: pl.BlockSpec(dims, lambda i: (0,) * len(dims))

    table_send = pl.pallas_call(
        table_kernel,
        out_shape=in_hbm(groups, GROUP, TILES * ROWS, L, BF16),
        compiler_params=PARAMS,
        name="table_send",
    )(value_table)
    table = exchange(table_send.reshape(OWNERS, TILES * ROWS, L), PLANE)

    batch_send, weights = pl.pallas_call(
        pack_kernel,
        grid=(GROUP // MANY,),
        in_specs=[
            whole(CANDS, TOK),
            whole(PICKS, TOK),
            whole(PICKS, TOK),
            pl.BlockSpec((TOK, MANY * WIDE), lambda i: (0, i)),
        ],
        out_specs=[pl.BlockSpec((MANY, WIDE + INFO, L), lambda i: (i, 0, 0)), whole(PICKS, TOK)],
        out_shape=(in_hbm(GROUP, WIDE + INFO, L, BF16), shape(PICKS, TOK, F32)),
        scratch_shapes=[pltpu.VMEM((INFO, TOK), BF16)],
        compiler_params=PARAMS,
        name="pack",
    )(owners.T, pick_index.T, key_scores.T, output_cotangent)
    batch = exchange(batch_send, TEAM)
    gain = lax.dynamic_slice(norm_gain, (block_index * WIDE,), (WIDE,)).reshape(WIDE, 1)

    batch_spec = pl.BlockSpec((STEP, WIDE + INFO, L), lambda i: (i, 0, 0))
    table_spec = whole(OWNERS, TILES * ROWS, L)
    wide_spec = pl.BlockSpec((WIDE, STEP * TOK), lambda i: (0, i))
    sums_spec = pl.BlockSpec((GROUP, 2, STEP * TOK), lambda i: (0, 0, i))
    tokens = GROUP * TOK

    vmem = pl.BlockSpec(memory_space=pltpu.VMEM)
    hbm = pl.BlockSpec(memory_space=pl.ANY)
    turned = pl.pallas_call(
        turn_kernel,
        in_specs=[vmem],
        out_specs=vmem,
        out_shape=shape(WIDE, TABLE, BF16),
        compiler_params=PARAMS,
        name="turn",
    )(table)
    memory, sums_send, placed = pl.pallas_call(
        forward_kernel,
        in_specs=[vmem] * 3,
        out_specs=[vmem] * 3,
        out_shape=(
            shape(WIDE, tokens, F32),
            shape(GROUP, 2, tokens, F32),
            shape(TABLE, tokens, BF16),
        ),
        compiler_params=PARAMS,
        name="forward",
    )(batch, turned, gain)
    sums = exchange(sums_send, TEAM)

    out_turned, memory_grad, grad_send = pl.pallas_call(
        backward_kernel,
        in_specs=[vmem] * 5,
        out_specs=[hbm, hbm, pl.BlockSpec()],
        out_shape=(
            in_hbm(WIDE, tokens, BF16),
            in_hbm(WIDE, tokens, BF16),
            in_hbm(OWNERS, GRAD, L, BF16),
        ),
        scratch_shapes=[
            pltpu.VMEM((WIDE, tokens), BF16),
            pltpu.VMEM((WIDE, tokens), BF16),
            pltpu.SemaphoreType.DMA((2,)),
        ],
        compiler_params=PARAMS,
        name="backward",
    )(batch, gain, memory, sums, placed)
    plane_parts = exchange(grad_send, PLANE)

    back_send = pl.pallas_call(
        placed_grad_kernel,
        grid=(steps,),
        in_specs=[batch_spec, table_spec, wide_spec, wide_spec],
        out_specs=pl.BlockSpec((STEP, BACK, L), lambda i: (i, 0, 0)),
        out_shape=in_hbm(GROUP, BACK, L, BF16),
        compiler_params=PARAMS,
        name="placed_grad",
    )(batch, table, out_turned, memory_grad)

    plane_parts, back_send = lax.optimization_barrier((plane_parts, back_send))
    shares_send = pl.pallas_call(
        plane_kernel,
        out_shape=shape(GROUP, GRAD, L, BF16),
        compiler_params=PARAMS,
        name="plane_sum",
    )(plane_parts.reshape(groups, GROUP, GRAD, L))
    shares = exchange(shares_send, "dp")
    total = pl.pallas_call(
        share_kernel,
        out_shape=shape(GRAD, L, BF16),
        compiler_params=PARAMS,
        name="share_sum",
    )(shares)
    total, back_send = lax.optimization_barrier((total, back_send))
    totals = lax.all_gather(total, "dp", axis=0, tiled=False)

    back = exchange(back_send, TEAM)
    rows_spec = pl.BlockSpec((ROWS, LAST * WIDE), lambda i: (0, i))
    memory_out, score_turned, new_table, new_first, new_second, gain_gradient = pl.pallas_call(
        last_kernel,
        grid=(GROUP // LAST,),
        in_specs=[
            pl.BlockSpec((LAST, BACK, L), lambda i: (i, 0, 0)),
            whole(PICKS, TOK),
            whole(PICKS, TOK),
            pl.BlockSpec((LAST, GRAD, L), lambda i: (i, 0, 0)),
            rows_spec,
            rows_spec,
            rows_spec,
        ],
        out_specs=[
            pl.BlockSpec((TOK, LAST * WIDE), lambda i: (0, i)),
            whole(PICKS, TOK),
            rows_spec,
            rows_spec,
            rows_spec,
            pl.BlockSpec((1, LAST * WIDE), lambda i: (0, i)),
        ],
        out_shape=(
            shape(TOK, D, BF16),
            shape(PICKS, TOK, F32),
            shape(ROWS, D, BF16),
            shape(ROWS, D, F32),
            shape(ROWS, D, F32),
            shape(1, D, F32),
        ),
        scratch_shapes=[pltpu.VMEM((SLOTS, TOK), F32)],
        compiler_params=PARAMS,
        name="last",
    )(back, pick_index.T, weights, totals, value_table, first_moment, second_moment)
    return (memory_out, score_turned.T, gain_gradient.reshape(D), new_table, new_first, new_second)


def solution(mesh):
    planes, mem_count = mesh.shape["dp"], mesh.shape["mem"]
    split_mesh = Mesh(mesh.devices.reshape(planes, mem_count // GROUP, PAIR, RING), ("dp",) + PLANE)
    tokens = P(("dp",) + PLANE, None)
    rows = P(PLANE, None)
    return jax.shard_map(
        per_device,
        mesh=split_mesh,
        in_specs=(tokens, tokens, tokens, tokens, rows, rows, rows, P()),
        out_specs=(tokens, tokens, P(), rows, rows, rows),
        check_vma=False,
    )
```
